512 devices in a mesh: ctx: 32 (over z, y_hi), tp: 8 (over x, y_lo), pool: 2 (over core).
Axes of the slice: x: 4, y: 4 (y_hi: 2, y_lo: 2; y = y_hi * 2 + y_lo), z: 16, core: 2. Of those that a mesh axis runs over, the one named last changes fastest.
Arguments:
- prompt_query: bfloat16 [2, 2, 4096, 8192], P('pool', None, 'ctx', 'tp'), may hold values from -32 to 32
- prompt_kv: bfloat16 [2, 2, 2, 4096, 1024], P('pool', None, None, 'ctx', 'tp'), may hold values from -12 to 12
- block_order: int32 [2, 2, 32], P('pool'), may hold values from 0 to 31, each once within a row
- decode_query: bfloat16 [2, 256, 2, 8192], P('pool', 'ctx', None, 'tp'), may hold values from -32 to 32
- history_kv: bfloat16 [2, 2, 256, 64, 1024], P('pool', None, 'ctx', None, 'tp'), may hold values from -5.5 to 5.5
- new_kv: bfloat16 [2, 2, 256, 2, 1024], P('pool', None, 'ctx', None, 'tp'), may hold values from -7 to 7
- hist_len: int32 [2, 256], P('pool', 'ctx'), may hold values from 1 to 64, as said below
- row_prompt: int32 [2, 256], P('pool', 'ctx'), may hold values from 0 to 1
Outputs:
- prefill_out: bfloat16 [2, 2, 4096, 8192], P('pool', None, ('ctx', 'tp'))
- decode_out: bfloat16 [2, 256, 2, 8192], P('pool', 'ctx', None, 'tp')
The draws below stay inside these ranges and needn't reach their ends.
Inputs may be any that keep to these rules, and one draw needn't show every extreme that they name: `block_order`: for each group and prompt every block index appears once. `hist_len`: every group has a row of length 64.
All inputs are finite; a program needn't handle non-finite values.
Results may differ from the reference program's by a relative error of at most 0.009.
Values may be sent and summed in bfloat16 or wider, within the bound.
A program may use at most 64 MiB of HBM per device.

```python
import math
import jax
import jax.numpy as jnp
from jax import lax

QUERY_HEADS = 64
KEY_VALUE_HEADS = 8
HEAD_SIZE = 128
PTOK = 128
PROMPT_COUNT = 2
HISTORY_TOKENS = 64
NEW_TOKENS = 2
GROUP_COUNT = 2
PROMPT_LENGTH = 4096
DECODE_ROW_COUNT = 256
N_CTX = 32


def clipped_gaussian(key, tensor_shape):
    return jax.random.truncated_normal(key, -4.0, 4.0, tensor_shape, jnp.float32)


def row_direction(key):
    return clipped_gaussian(jax.random.fold_in(key, 202), (GROUP_COUNT, DECODE_ROW_COUNT, KEY_VALUE_HEADS * HEAD_SIZE))


def spread_heads(vector_rows):
    leading_dimensions = vector_rows.shape[:-1]
    each_head = vector_rows.reshape(leading_dimensions + (KEY_VALUE_HEADS, 1, HEAD_SIZE))
    return jnp.broadcast_to(each_head, leading_dimensions + (KEY_VALUE_HEADS, QUERY_HEADS // KEY_VALUE_HEADS, HEAD_SIZE)).reshape(leading_dimensions + (QUERY_HEADS * HEAD_SIZE,))


def draw_prompt_query(key, part):
    key = jax.random.fold_in(key, 1)
    tensor_shape = (GROUP_COUNT, PROMPT_COUNT, PROMPT_LENGTH, QUERY_HEADS * HEAD_SIZE)
    drawn = clipped_gaussian(key, tensor_shape)
    return drawn.astype(jnp.bfloat16)


def draw_prompt_kv(key, part):
    key = jax.random.fold_in(key, 2)
    tensor_shape = (GROUP_COUNT, 2, PROMPT_COUNT, PROMPT_LENGTH, KEY_VALUE_HEADS * HEAD_SIZE)
    drawn = clipped_gaussian(key, tensor_shape)
    return drawn.astype(jnp.bfloat16)


def draw_decode_query(key, part):
    guide = row_direction(key)
    key = jax.random.fold_in(key, 3)
    tensor_shape = (GROUP_COUNT, DECODE_ROW_COUNT, NEW_TOKENS, QUERY_HEADS * HEAD_SIZE)
    shared = spread_heads(guide)[:, :, None, :]
    drawn = 2.5 * clipped_gaussian(key, tensor_shape) + shared
    return drawn.astype(jnp.bfloat16)


def draw_history_kv(key, part):
    guide = row_direction(key)
    key = jax.random.fold_in(key, 4)
    tensor_shape = (GROUP_COUNT, 2, DECODE_ROW_COUNT, HISTORY_TOKENS, KEY_VALUE_HEADS * HEAD_SIZE)
    drawn = clipped_gaussian(key, tensor_shape)
    key_part = drawn[:, 0] + 0.33 * guide[:, :, None, :]
    return jnp.stack([key_part, drawn[:, 1]], axis=1).astype(jnp.bfloat16)


def draw_new_kv(key, part):
    guide = row_direction(key)
    key = jax.random.fold_in(key, 5)
    tensor_shape = (GROUP_COUNT, 2, DECODE_ROW_COUNT, NEW_TOKENS, KEY_VALUE_HEADS * HEAD_SIZE)
    drawn = clipped_gaussian(key, tensor_shape)
    key_part = drawn[:, 0] + 0.65 * guide[:, :, None, :]
    return jnp.stack([key_part, drawn[:, 1]], axis=1).astype(jnp.bfloat16)


def draw_hist_len(key, part):
    key = jax.random.fold_in(key, 6)
    first_key, second_key = jax.random.split(key)
    lengths = jax.random.randint(first_key, (GROUP_COUNT, DECODE_ROW_COUNT), 1, HISTORY_TOKENS + 1, jnp.int32)
    chosen = jax.random.randint(second_key, (GROUP_COUNT, 1), 0, DECODE_ROW_COUNT, jnp.int32)
    return jnp.where(jnp.arange(DECODE_ROW_COUNT, dtype=jnp.int32)[None, :] == chosen, HISTORY_TOKENS, lengths).astype(jnp.int32)


def with_ends(values, stream_key, least, top_value):
    longest = values.shape.index(max(values.shape))
    spots = []
    for shift in (0, 1):
        where = [jax.random.randint(jax.random.fold_in(stream_key, axis), (), 0, length) for axis, length in enumerate(values.shape)]
        where[longest] = (where[longest] + shift) % values.shape[longest]
        spots.append(tuple(where))
    return values.at[spots[0]].set(least).at[spots[1]].set(top_value)


def setup_inputs(seed: int = 0) -> dict:
    key_list = jax.random.split(jax.random.key(seed), 9)
    prompt_query = draw_prompt_query(jax.random.fold_in(key_list[8], 71), 0)
    prompt_kv = draw_prompt_kv(jax.random.fold_in(key_list[8], 71), 0)
    block_order = jax.vmap(lambda own: jax.random.permutation(own, N_CTX))(jax.random.split(key_list[2], GROUP_COUNT * PROMPT_COUNT)).reshape((GROUP_COUNT, PROMPT_COUNT, N_CTX)).astype(jnp.int32)
    decode_query = draw_decode_query(jax.random.fold_in(key_list[8], 71), 0)
    history_kv = draw_history_kv(jax.random.fold_in(key_list[8], 71), 0)
    new_kv = draw_new_kv(jax.random.fold_in(key_list[8], 71), 0)
    hist_len = draw_hist_len(jax.random.fold_in(key_list[8], 71), 0)
    row_prompt = with_ends(jax.random.randint(key_list[7], (GROUP_COUNT, DECODE_ROW_COUNT), 0, PROMPT_COUNT), jax.random.fold_in(key_list[7], 1), 0, PROMPT_COUNT - 1).astype(jnp.int32)
    return dict(prompt_query=prompt_query, prompt_kv=prompt_kv, block_order=block_order, decode_query=decode_query, history_kv=history_kv, new_kv=new_kv, hist_len=hist_len, row_prompt=row_prompt)


NEG = -1e30


def rounded(values):
    return lax.optimization_barrier(values.astype(jnp.bfloat16)).astype(jnp.float32)


def head_attend(query_rows, rows_of_keys, rows_of_values, visible):
    scaling = HEAD_SIZE ** -0.5
    scores = jnp.einsum('gnd,md->gnm', query_rows, rows_of_keys) * scaling
    highest = jnp.max(jnp.where(visible[None], scores, NEG), axis=-1, keepdims=True)
    weights = jnp.where(visible[None], jnp.exp(scores - highest), 0.0)
    weight_sum = jnp.sum(weights, axis=-1, keepdims=True)
    weighted = jnp.einsum('gnm,md->gnd', rounded(weights), rows_of_values)
    return weighted / weight_sum


def prefill_one(query_rows, rows_of_keys, rows_of_values, order_row):
    group_width = QUERY_HEADS // KEY_VALUE_HEADS
    row_ids = jnp.arange(PROMPT_LENGTH, dtype=jnp.int32)
    positions = order_row.astype(jnp.int32)[row_ids // PTOK] * PTOK + row_ids % PTOK
    step_spacing = math.gcd(PROMPT_LENGTH, 512)
    blocks_of_queries = query_rows.astype(jnp.float32).reshape(PROMPT_LENGTH // step_spacing, step_spacing, KEY_VALUE_HEADS, group_width, HEAD_SIZE)
    heads_of_keys = rows_of_keys.astype(jnp.float32).reshape(PROMPT_LENGTH, KEY_VALUE_HEADS, HEAD_SIZE)
    heads_of_values = rows_of_values.astype(jnp.float32).reshape(PROMPT_LENGTH, KEY_VALUE_HEADS, HEAD_SIZE)
    position_blocks = positions.reshape(PROMPT_LENGTH // step_spacing, step_spacing)

    def per_block(block_item):
        query_block, block_positions = block_item
        visible = positions[None, :] <= block_positions[:, None]

        def each_head(head_index):
            head_queries = jnp.transpose(query_block[:, head_index], (1, 0, 2))
            return head_attend(head_queries, heads_of_keys[:, head_index], heads_of_values[:, head_index], visible)

        output_rows = lax.map(each_head, jnp.arange(KEY_VALUE_HEADS, dtype=jnp.int32))
        return jnp.transpose(output_rows, (2, 0, 1, 3)).reshape(step_spacing, QUERY_HEADS * HEAD_SIZE)

    result = lax.map(per_block, (blocks_of_queries, position_blocks))
    return result.reshape(PROMPT_LENGTH, QUERY_HEADS * HEAD_SIZE).astype(jnp.bfloat16)


def decode_group(query_rows, prompt_key_rows, prompt_value_rows, history_keys, history_values, fresh_keys, fresh_values, lengths, owner_prompt):
    group_width = QUERY_HEADS // KEY_VALUE_HEADS
    scaling = HEAD_SIZE ** -0.5
    heads_of_queries = query_rows.astype(jnp.float32).reshape(DECODE_ROW_COUNT, NEW_TOKENS, KEY_VALUE_HEADS, group_width, HEAD_SIZE)
    prompt_heads_keys = prompt_key_rows.astype(jnp.float32).reshape(PROMPT_COUNT, PROMPT_LENGTH, KEY_VALUE_HEADS, HEAD_SIZE)
    prompt_heads_values = prompt_value_rows.astype(jnp.float32).reshape(PROMPT_COUNT, PROMPT_LENGTH, KEY_VALUE_HEADS, HEAD_SIZE)
    history_key_heads = history_keys.astype(jnp.float32).reshape(DECODE_ROW_COUNT, HISTORY_TOKENS, KEY_VALUE_HEADS, HEAD_SIZE)
    history_value_heads = history_values.astype(jnp.float32).reshape(DECODE_ROW_COUNT, HISTORY_TOKENS, KEY_VALUE_HEADS, HEAD_SIZE)
    fresh_key_heads = fresh_keys.astype(jnp.float32).reshape(DECODE_ROW_COUNT, NEW_TOKENS, KEY_VALUE_HEADS, HEAD_SIZE)
    fresh_value_heads = fresh_values.astype(jnp.float32).reshape(DECODE_ROW_COUNT, NEW_TOKENS, KEY_VALUE_HEADS, HEAD_SIZE)
    prompt_mask = (owner_prompt.astype(jnp.int32)[:, None] == jnp.arange(PROMPT_COUNT, dtype=jnp.int32)[None, :])[:, None, None, :, None]
    hist_mask = (jnp.arange(HISTORY_TOKENS, dtype=jnp.int32)[None, :] < lengths.astype(jnp.int32)[:, None])[:, None, None, :]
    new_mask = (jnp.arange(NEW_TOKENS, dtype=jnp.int32)[None, :] <= jnp.arange(NEW_TOKENS, dtype=jnp.int32)[:, None])[None, :, None, :]

    def each_head(head_index):
        head_queries = heads_of_queries[:, :, head_index]
        prompt_scores = jnp.einsum('rsgd,pld->rsgpl', head_queries, prompt_heads_keys[:, :, head_index]) * scaling
        hist_scores = jnp.einsum('rsgd,rjd->rsgj', head_queries, history_key_heads[:, :, head_index]) * scaling
        new_scores = jnp.einsum('rsgd,rud->rsgu', head_queries, fresh_key_heads[:, :, head_index]) * scaling
        highest = jnp.maximum(jnp.max(jnp.where(prompt_mask, prompt_scores, NEG), axis=(-2, -1)),
                              jnp.maximum(jnp.max(jnp.where(hist_mask, hist_scores, NEG), axis=-1),
                                          jnp.max(jnp.where(new_mask, new_scores, NEG), axis=-1)))
        prompt_weights = jnp.where(prompt_mask, jnp.exp(prompt_scores - highest[..., None, None]), 0.0)
        hist_weights = jnp.where(hist_mask, jnp.exp(hist_scores - highest[..., None]), 0.0)
        new_weights = jnp.where(new_mask, jnp.exp(new_scores - highest[..., None]), 0.0)
        weight_sum = jnp.sum(prompt_weights, axis=(-2, -1)) + jnp.sum(hist_weights, axis=-1) + jnp.sum(new_weights, axis=-1)
        weighted = jnp.einsum('rsgpl,pld->rsgd', rounded(prompt_weights), prompt_heads_values[:, :, head_index])
        weighted = weighted + jnp.einsum('rsgj,rjd->rsgd', rounded(hist_weights), history_value_heads[:, :, head_index])
        weighted = weighted + jnp.einsum('rsgu,rud->rsgd', rounded(new_weights), fresh_value_heads[:, :, head_index])
        return weighted / weight_sum[..., None]

    output_rows = lax.map(each_head, jnp.arange(KEY_VALUE_HEADS, dtype=jnp.int32))
    return jnp.transpose(output_rows, (1, 2, 0, 3, 4)).reshape(DECODE_ROW_COUNT, NEW_TOKENS, QUERY_HEADS * HEAD_SIZE).astype(jnp.bfloat16)


def reference(prompt_query, prompt_kv, block_order, decode_query, history_kv, new_kv, hist_len, row_prompt):
    prefilled = []
    for group_index in range(GROUP_COUNT):
        per_prompt = [prefill_one(prompt_query[group_index, prompt_index], prompt_kv[group_index, 0, prompt_index],
                                  prompt_kv[group_index, 1, prompt_index], block_order[group_index, prompt_index])
                      for prompt_index in range(PROMPT_COUNT)]
        prefilled.append(jnp.stack(per_prompt))
    decoded = []
    for group_index in range(GROUP_COUNT):
        other_group = GROUP_COUNT - 1 - group_index
        decoded.append(decode_group(decode_query[group_index], prompt_kv[other_group, 0], prompt_kv[other_group, 1],
                                    history_kv[group_index, 0], history_kv[group_index, 1],
                                    new_kv[group_index, 0], new_kv[group_index, 1],
                                    hist_len[group_index], row_prompt[group_index]))
    return jnp.stack(prefilled), jnp.stack(decoded)
```

```python
import functools

import jax
import jax.numpy as jnp
from jax import lax
from jax.experimental import pallas as pl
from jax.experimental.pallas import tpu as pltpu
from jax.sharding import PartitionSpec as P

HEAD_SIZE = 128
NEG = -1e30
SCALE = 1.4426950408889634 / HEAD_SIZE**0.5
NT = (((1,), (1,)), ((), ()))
TN = (((0,), (0,)), ((), ()))
MESH = pl.DeviceIdType.MESH
EARLY = 2
ONES = 16


def kernel(
    half,
    tps,
    order,
    hist_len,
    row_prompt,
    pq,
    pkv,
    dq,
    hist,
    new,
    out,
    dout,
    buf,
    psend,
    q1,
    dqs,
    dqr,
    acc,
    top,
    stage,
    dstage,
    din,
    dloc,
    ring_send,
    ring_recv,
    x_send,
    x_recv,
    q_send,
    q_recv,
    d_send,
    d_recv,
    r_send,
    r_recv,
    o_send,
    o_recv,
    o_local,
):
    ctx, tp, core = lax.axis_index("ctx"), lax.axis_index("tp"), lax.axis_index("pool")
    zs = 2 * half
    z, yh = ctx // 2, ctx % 2
    rows = 128 // tps

    def dev(z_, yh_, tp_, core_):
        return {"ctx": z_ * 2 + yh_, "tp": tp_, "pool": core_}

    right = dev(lax.rem(z + 1, zs), yh, tp, core)
    left = dev(lax.rem(z + zs - 1, zs), yh, tp, core)
    partner = dev(z, 1 - yh, tp, core)
    helpers = (dev(z, yh, tp, 1 - core), dev(z, 1 - yh, tp, 1 - core))

    def other_tp(k):
        return lax.rem(tp + k, tps)

    owners = [[dev(z, yh, other_tp(k), core) for k in range(tps)], [dev(z, 1 - yh, other_tp(k), core) for k in range(tps)]]

    def remote(src, dst, send, recv, device):
        return pltpu.make_async_remote_copy(
            src_ref=src, dst_ref=dst, send_sem=send, recv_sem=recv, device_id=device, device_id_type=MESH
        )

    barrier = pltpu.get_barrier_semaphore()
    peers = [right, left, *helpers, *owners[0][1:], *owners[1]]
    for peer in peers:
        pl.semaphore_signal(barrier, inc=1, device_id=peer, device_id_type=MESH)

    def slab(dst, prompt):
        dst[0:128, :] = pkv[0, 0, prompt]
        dst[128:256, :] = pkv[0, 1, prompt].astype(jnp.float32).T.astype(jnp.bfloat16)

    slab(buf.at[0, 0], yh)
    slab(psend, 1 - yh)
    heads = [dq[:, h * 128 : (h + 1) * 128] for h in range(8)]
    dqt = jnp.concatenate(heads, axis=0)
    dqs[...] = dqt
    pl.semaphore_wait(barrier, len(peers))

    def ring(k, c, src=None):
        return remote(
            buf.at[k - 1, c] if src is None else src,
            buf.at[k, c],
            ring_send.at[k, c],
            ring_recv.at[k, c],
            right if c < 2 else left,
        )

    x_copy = remote(psend, buf.at[0, 1], x_send, x_recv, partner)
    q_copies = [
        remote(pq.at[0, 1 - yh, :, t * 256 : (t + 1) * 256], q1.at[t], q_send.at[t], q_recv.at[t], partner)
        for t in range(4)
    ]
    d_copies = [remote(dqs, dqr.at[i], d_send.at[i], d_recv.at[i], helpers[i]) for i in range(2)]
    x_copy.start()
    ring(1, 0).start()
    ring(1, 2, buf.at[0, 0]).start()
    for copy in d_copies + q_copies:
        copy.start()

    def event(k, c):
        ring(k, c).wait_recv()
        if c in (0, 3):

            @pl.when(k < half)
            def _():
                ring(k + 1, c).start()

        else:

            @pl.when(k + 1 < half)
            def _():
                ring(k + 1, c).start()

    lane = lax.broadcasted_iota(jnp.int32, (1, 128), 1)
    lane_row, lane_step = lax.rem(lane, 16) // 2, lax.rem(lane, 2)
    hs = lax.dot_general(hist[0, 0].reshape(512, 128), dqt, NT, preferred_element_type=jnp.float32) * SCALE
    key_in_row = lax.broadcasted_iota(jnp.int32, (64, 128), 0)
    hs = jnp.concatenate(
        [
            jnp.where((lane_row == r) & (key_in_row < hist_len[0, r]), hs[r * 64 : (r + 1) * 64], NEG)
            for r in range(8)
        ],
        axis=0,
    )
    ns = lax.dot_general(new[0], dqt, NT, preferred_element_type=jnp.float32) * SCALE
    key = lax.broadcasted_iota(jnp.int32, (16, 128), 0)
    ns = jnp.where((key // 2 == lane_row) & (lax.rem(key, 2) <= lane_step), ns, NEG)
    highest = jnp.maximum(jnp.max(hs, axis=0, keepdims=True), jnp.max(ns, axis=0, keepdims=True))
    hw, nw = jnp.exp2(hs - highest), jnp.exp2(ns - highest)
    weighted = lax.dot_general(
        hist[0, 1].reshape(512, 128), hw.astype(jnp.bfloat16), TN, preferred_element_type=jnp.float32
    ) + lax.dot_general(new[1], nw.astype(jnp.bfloat16), TN, preferred_element_type=jnp.float32)
    dloc[0:128] = weighted
    dloc[128:136] = jnp.broadcast_to(jnp.sum(hw, 0, keepdims=True) + jnp.sum(nw, 0, keepdims=True), (8, 128))
    dloc[136:144] = jnp.broadcast_to(highest, (8, 128))

    def queries(t):
        if t == 8:
            return dqr[...].reshape(256, 128)
        x = pq[0, yh, :, t * 256 : (t + 1) * 256] if t < 4 else q1[t - 4]
        return jnp.concatenate([x[:, :128], x[:, 128:]], axis=0)

    causal = lax.rem(lax.broadcasted_iota(jnp.int32, (128, 256), 1), 128) >= lax.broadcasted_iota(
        jnp.int32, (128, 256), 0
    )

    def place(z_, yh_):
        return order[0, yh, lax.rem(z_ + zs, zs) * 2 + yh_]

    own_place = (place(z, yh), place(z, 1 - yh))

    def attend(tiles, u, chunks, sources, first=False):
        keys = jnp.concatenate([buf[u, c, 0:128, :] for c in chunks], axis=0)
        values = jnp.concatenate(
            [
                jnp.concatenate([buf[u, c, 128:256, :] for c in chunks], axis=1),
                jnp.ones((ONES, 128 * len(chunks)), jnp.bfloat16),
            ],
            axis=0,
        )
        places = [place(*s) for s in sources]
        bias = [[jnp.where(pk <= own_place[i], 0.0, NEG).astype(jnp.float32) for pk in places] for i in range(2)]

        def scores(t):
            return lax.dot_general(keys, queries(t), NT, preferred_element_type=jnp.float32)

        def weights(t, s):
            s = s * SCALE
            parts = [s[i * 128 : (i + 1) * 128] for i in range(len(chunks))]
            shift = [None] * len(chunks)
            if t < 8:
                shift = list(bias[t // 4])
                if first:
                    shift[t // 4] = None
                    parts[t // 4] = jnp.where(causal, parts[t // 4], NEG)
            tops = [jnp.max(x, axis=0, keepdims=True) for x in parts]
            tops = [x if b is None else x + b for x, b in zip(tops, shift)]
            now = functools.reduce(jnp.maximum, tops)
            factor = None
            if not first:
                before = top[t, 0:1]
                now = jnp.maximum(now, before)
                factor = jnp.exp2(before - now)
            top[t, 0:1] = now
            w = [jnp.exp2(x - (now if b is None else now - b)).astype(jnp.bfloat16) for x, b in zip(parts, shift)]
            return jnp.concatenate(w, axis=0), factor

        def add(t, w, factor):
            o = jnp.dot(values, w, preferred_element_type=jnp.float32)
            acc[t] = o if factor is None else acc[t] * factor + o

        s = {i: scores(tiles[i]) for i in range(min(2, len(tiles)))}
        w = {0: weights(tiles[0], s[0])}
        for i in range(len(tiles)):
            if i + 2 < len(tiles):
                s[i + 2] = scores(tiles[i + 2])
            if i + 1 < len(tiles):
                w[i + 1] = weights(tiles[i + 1], s[i + 1])
            add(tiles[i], *w[i])

    def step_sources(k):
        return [(z - k, yh), (z - k, 1 - yh), (z + k, yh), (z + k, 1 - yh)]

    def own(tiles):
        attend(tiles, 0, (0, 1), [(z, yh), (z, 1 - yh)], first=True)

    def step(k, tiles):
        attend(tiles, k, (0, 1, 2, 3), step_sources(k))

    x_copy.wait_recv()
    ring(1, 1).start()
    ring(1, 3, buf.at[0, 1]).start()
    own([0, 1, 2, 3])
    event(1, 0)
    event(1, 2)
    for copy in d_copies:
        copy.wait_recv()
    own([8])
    event(1, 1)
    event(1, 3)

    early = min(EARLY, half - 2)

    def early_step(k, _):
        step(k, [0, 1, 2])
        event(k + 1, 0)
        event(k + 1, 2)
        step(k, [3, 8])
        event(k + 1, 1)
        event(k + 1, 3)
        return 0

    lax.fori_loop(1, early + 1, early_step, 0)
    for copy in q_copies:
        copy.wait_recv()
    own([4, 5, 6, 7])

    def middle_step(k, _):
        step(k, [0, 1, 2, 3, 4, 5, 6])
        event(k + 1, 0)
        event(k + 1, 2)
        step(k, [7, 8])
        step(k - early, [4, 5, 6, 7])
        event(k + 1, 1)
        event(k + 1, 3)
        return 0

    middle_end = min(2 * early + 1, half - 1)
    lax.fori_loop(early + 1, middle_end, middle_step, 0)

    def late_step(k, _):
        step(k, [8, 4, 5, 6])
        event(k + 1, 0)

        @pl.when(k + 1 < half)
        def _():
            event(k + 1, 2)

        step(k, [7, 0, 1, 2, 3])

        @pl.when(k + 1 < half)
        def _():
            event(k + 1, 1)

        event(k + 1, 3)
        return 0

    for u in range(middle_end - early, early + 1):
        step(u, [4, 5, 6, 7])
    lax.fori_loop(middle_end, half, late_step, 0)

    far = [(z - half, yh), (z + half, 1 - yh)]
    attend([8, 4, 5, 6, 7, 0, 1, 2, 3], half, (0, 3), far)
    r_copies = []
    for i in range(2):
        dstage[i, 0:136] = acc[8, 0:136, i * 128 : (i + 1) * 128]
        dstage[i, 136:144] = jnp.broadcast_to(top[8, 0:1, i * 128 : (i + 1) * 128], (8, 128))
        r_copies.append(remote(dstage.at[i], din.at[yh], r_send.at[i], r_recv.at[i], helpers[i]))
        r_copies[i].start()

    o_copies = []
    for item in (1, 0):
        for t in range(4):
            a = acc[item * 4 + t]
            o = a[0:128] / a[128:129]
            for h in range(2):
                col = (2 * t + h) * 128
                stage[item, :, col : col + 128] = o[:, h * 128 : (h + 1) * 128].T.astype(jnp.bfloat16)
        for k in range(tps):
            src = stage.at[item, pl.ds(pl.multiple_of(other_tp(k) * rows, rows), rows), :]
            dst = out.at[0, yh, :, pl.ds(pl.multiple_of(tp * 1024, 1024), 1024)]
            if item == 0 and k == 0:
                local = pltpu.make_async_copy(src, dst, o_local)
                local.start()
            else:
                o_copies.append(remote(src, dst, o_send.at[item, k], o_recv.at[item, k], owners[item][k]))
                o_copies[-1].start()

    for copy in r_copies:
        copy.wait_recv()
    wanted = jnp.zeros((1, 128), jnp.int32)
    for r in range(8):
        wanted = jnp.where(lane_row == r, row_prompt[0, r], wanted)
    shared = jnp.where(wanted == 1, din[1], din[0])
    highest = jnp.maximum(shared[136:137], dloc[136:137])
    fa, fb = jnp.exp2(shared[136:137] - highest), jnp.exp2(dloc[136:137] - highest)
    total = shared[128:129] * fa + dloc[128:129] * fb
    o = ((shared[0:128] * fa + dloc[0:128] * fb) / total).T.astype(jnp.bfloat16)
    for h in range(8):
        dout[:, h * 128 : (h + 1) * 128] = o[h * 16 : (h + 1) * 16]

    local.wait()
    for copy in o_copies:
        copy.wait_recv()
    x_copy.wait_send()
    for copy in d_copies + q_copies + r_copies + o_copies:
        copy.wait_send()
    for c in range(4):

        def drain(k, _, c=c):
            ring(k, c).wait_send()
            return 0

        lax.fori_loop(1, half + 1 if c in (0, 3) else half, drain, 0)


def per_device(zs, tps, prompt_query, prompt_kv, block_order, decode_query, history_kv, new_kv, hist_len, row_prompt):
    half = zs // 2
    rows = 128 // tps
    vmem = pl.BlockSpec(memory_space=pltpu.VMEM)
    smem = pl.BlockSpec(memory_space=pltpu.SMEM)
    dma = pltpu.SemaphoreType.DMA
    prefill_out, decode_out = pl.pallas_call(
        functools.partial(kernel, half, tps),
        out_shape=(
            jax.ShapeDtypeStruct((1, 2, rows, 1024 * tps), jnp.bfloat16),
            jax.ShapeDtypeStruct((16, 1024), jnp.bfloat16),
        ),
        in_specs=[smem] * 3 + [vmem] * 5,
        out_specs=(pl.BlockSpec(memory_space=pl.ANY), vmem),
        scratch_shapes=[
            pltpu.VMEM((half + 1, 4, 256, 128), jnp.bfloat16),
            pltpu.VMEM((256, 128), jnp.bfloat16),
            pltpu.VMEM((4, 128, 256), jnp.bfloat16),
            pltpu.VMEM((128, 128), jnp.bfloat16),
            pltpu.VMEM((2, 128, 128), jnp.bfloat16),
            pltpu.VMEM((9, 128 + ONES, 256), jnp.float32),
            pltpu.VMEM((9, 8, 256), jnp.float32),
            pltpu.VMEM((2, 128, 1024), jnp.bfloat16),
            pltpu.VMEM((2, 144, 128), jnp.float32),
            pltpu.VMEM((2, 144, 128), jnp.float32),
            pltpu.VMEM((144, 128), jnp.float32),
            dma((half + 1, 4)),
            dma((half + 1, 4)),
            dma(()),
            dma(()),
            dma((4,)),
            dma((4,)),
            dma((2,)),
            dma((2,)),
            dma((2,)),
            dma((2,)),
            dma((2, tps)),
            dma((2, tps)),
            dma(()),
        ],
        compiler_params=pltpu.CompilerParams(
            collective_id=0, has_side_effects=True, vmem_limit_bytes=48 << 20
        ),
    )(
        block_order,
        hist_len,
        row_prompt,
        prompt_query,
        prompt_kv,
        decode_query.reshape(16, 1024),
        history_kv,
        new_kv.reshape(2, 16, 128),
    )
    return prefill_out, decode_out.reshape(decode_query.shape)


def solution(mesh):
    placed = (
        P("pool", None, "ctx", "tp"),
        P("pool", None, None, "ctx", "tp"),
        P("pool", None, None),
        P("pool", "ctx", None, "tp"),
        P("pool", None, "ctx", None, "tp"),
        P("pool", None, "ctx", None, "tp"),
        P("pool", "ctx"),
        P("pool", "ctx"),
    )
    return jax.shard_map(
        functools.partial(per_device, mesh.shape["ctx"] // 2, mesh.shape["tp"]),
        mesh=mesh,
        in_specs=placed,
        out_specs=(P("pool", None, ("ctx", "tp"), None), P("pool", "ctx", None, "tp")),
        check_vma=False,
    )
```

```python
import functools

import jax
import jax.numpy as jnp
from jax import lax
from jax.experimental import pallas as pl
from jax.experimental.pallas import tpu as pltpu
from jax.sharding import PartitionSpec as P

HEAD_SIZE = 128
NEG = -1e30
SCALE = 1.4426950408889634 / HEAD_SIZE**0.5
NT = (((1,), (1,)), ((), ()))
TN = (((0,), (0,)), ((), ()))
MESH = pl.DeviceIdType.MESH
ONES = 16


def kernel(
    half,
    tps,
    order_in,
    hist_len_in,
    row_prompt_in,
    pq,
    pkv_in,
    dq_in,
    hist_in,
    new_in,
    out,
    dout,
    order,
    hist_len,
    row_prompt,
    q0,
    raw,
    dq,
    hist,
    new,
    buf,
    psend,
    q1,
    dqs,
    dqr,
    acc,
    top,
    stage,
    dstage,
    din,
    dloc,
    in_sem,
    ring_send,
    ring_recv,
    x_send,
    x_recv,
    near_send,
    q_send,
    q_recv,
    d_send,
    d_recv,
    r_send,
    r_recv,
    o_send,
    o_recv,
    o_local,
):
    ctx, tp, core = lax.axis_index("ctx"), lax.axis_index("tp"), lax.axis_index("pool")
    zs = 2 * half
    z, yh = ctx // 2, ctx % 2
    rows = 128 // tps

    def dev(z_, yh_, tp_, core_):
        return {"ctx": lax.rem(z_ + zs, zs) * 2 + yh_, "tp": tp_, "pool": core_}

    right, left = dev(z + 1, yh, tp, core), dev(z - 1, yh, tp, core)
    partner = dev(z, 1 - yh, tp, core)
    partner_right, partner_left = dev(z + 1, 1 - yh, tp, core), dev(z - 1, 1 - yh, tp, core)
    helpers = (dev(z, yh, tp, 1 - core), dev(z, 1 - yh, tp, 1 - core))

    def other_tp(k):
        return lax.rem(tp + k, tps)

    owners = [[dev(z, yh, other_tp(k), core) for k in range(tps)], [dev(z, 1 - yh, other_tp(k), core) for k in range(tps)]]

    def remote(src, dst, send, recv, device):
        return pltpu.make_async_remote_copy(
            src_ref=src, dst_ref=dst, send_sem=send, recv_sem=recv, device_id=device, device_id_type=MESH
        )

    barrier = pltpu.get_barrier_semaphore()
    peers = [right, left, partner_right, partner_left, *helpers, *owners[0][1:], *owners[1]]
    for peer in peers:
        pl.semaphore_signal(barrier, inc=1, device_id=peer, device_id_type=MESH)

    fetches = [
        pltpu.make_async_copy(src, dst, in_sem.at[i])
        for i, (src, dst) in enumerate(
            [
                (pkv_in.at[0, 1], raw),
                (dq_in.at[0], dq),
                (pkv_in.at[0, 0, yh], buf.at[0, 0, 0:128]),
                (hist_len_in, hist_len),
                (hist_in.at[0], hist),
                (new_in, new),
                (order_in, order),
                (row_prompt_in, row_prompt),
                (pq.at[0, yh], q0),
            ]
        )
    ]
    for fetch in fetches:
        fetch.start()
    pl.semaphore_wait(barrier, len(peers))

    def part(ref, h):
        return ref.at[h * 128 : (h + 1) * 128]

    def ring(k, c, h, src=None):
        return remote(
            part(buf.at[k - 1, c], h) if src is None else src,
            part(buf.at[k, c], h),
            ring_send.at[k, c, h],
            ring_recv.at[k, c, h],
            right if c < 2 else left,
        )

    mine = (pkv_in.at[0, 0, yh], part(buf.at[0, 0], 1))
    theirs = (pkv_in.at[0, 0, 1 - yh], psend)
    x_copies = [remote(theirs[h], part(buf.at[0, 1], h), x_send.at[h], x_recv.at[h], partner) for h in range(2)]
    near_copies = [
        [
            remote(theirs[h], part(buf.at[1, c], h), near_send.at[i, h], ring_recv.at[1, c, h], device)
            for i, (c, device) in enumerate([(1, partner_right), (3, partner_left)])
        ]
        for h in range(2)
    ]
    q_copy = remote(pq.at[0, 1 - yh], q1, q_send, q_recv, partner)
    d_copies = [remote(dqs, dqr.at[i], d_send.at[i], d_recv.at[i], helpers[i]) for i in range(2)]
    def send_own(h):
        for copy in [ring(1, 0, h, mine[h]), ring(1, 2, h, mine[h]), *near_copies[h], x_copies[h]]:
            copy.start()

    send_own(0)
    fetches[0].wait()
    buf[0, 0, 128:256, :] = raw[yh].astype(jnp.float32).T.astype(jnp.bfloat16)
    psend[...] = raw[1 - yh].astype(jnp.float32).T.astype(jnp.bfloat16)
    send_own(1)
    fetches[1].wait()
    wide = dq[...].astype(jnp.float32).reshape(16, 1024)
    dqt = jnp.concatenate([wide[:, h * 128 : (h + 1) * 128] for h in range(8)], axis=0).astype(jnp.bfloat16)
    dqs[...] = dqt
    for copy in d_copies:
        copy.start()
    for fetch in fetches[2:]:
        fetch.wait()

    lane = lax.broadcasted_iota(jnp.int32, (1, 128), 1)
    lane_row, lane_step = lax.rem(lane, 16) // 2, lax.rem(lane, 2)
    hs = lax.dot_general(hist[0].reshape(512, 128), dqt, NT, preferred_element_type=jnp.float32) * SCALE
    key_in_row = lax.broadcasted_iota(jnp.int32, (64, 128), 0)
    hs = jnp.concatenate(
        [
            jnp.where((lane_row == r) & (key_in_row < hist_len[0, r]), hs[r * 64 : (r + 1) * 64], NEG)
            for r in range(8)
        ],
        axis=0,
    )
    ns = lax.dot_general(new[0], dqt, NT, preferred_element_type=jnp.float32) * SCALE
    key = lax.broadcasted_iota(jnp.int32, (16, 128), 0)
    ns = jnp.where((key // 2 == lane_row) & (lax.rem(key, 2) <= lane_step), ns, NEG)
    highest = jnp.maximum(jnp.max(hs, axis=0, keepdims=True), jnp.max(ns, axis=0, keepdims=True))
    hw, nw = jnp.exp2(hs - highest), jnp.exp2(ns - highest)
    weighted = lax.dot_general(
        hist[1].reshape(512, 128), hw.astype(jnp.bfloat16), TN, preferred_element_type=jnp.float32
    ) + lax.dot_general(new[1], nw.astype(jnp.bfloat16), TN, preferred_element_type=jnp.float32)
    dloc[0:128] = weighted
    dloc[128:136] = jnp.broadcast_to(jnp.sum(hw, 0, keepdims=True) + jnp.sum(nw, 0, keepdims=True), (8, 128))
    dloc[136:144] = jnp.broadcast_to(highest, (8, 128))

    def event(k, b, h, last=0):
        for c in (b, b + 2):
            if last < 2 or c in (0, 3):
                ring(k, c, h).wait_recv()
                if last == 0 or (last == 1 and c in (0, 3)):
                    ring(k + 1, c, h).start()

    def queries(t):
        if t == 8:
            return dqr[...].reshape(256, 128)
        x = (q0 if t < 4 else q1)[:, t % 4 * 256 : (t % 4 + 1) * 256]
        return jnp.concatenate([x[:, :128], x[:, 128:]], axis=0)

    causal = lax.rem(lax.broadcasted_iota(jnp.int32, (128, 256), 1), 128) >= lax.broadcasted_iota(
        jnp.int32, (128, 256), 0
    )

    def place(z_, yh_):
        return order[0, yh, lax.rem(z_ + zs, zs) * 2 + yh_]

    own_place = (place(z, yh), place(z, 1 - yh))

    def attend(tiles, u, chunks, sources, first=False, between=()):
        between = dict(between)
        keys = jnp.concatenate([buf[u, c, 0:128, :] for c in chunks], axis=0)
        values = jnp.concatenate(
            [
                jnp.concatenate([buf[u, c, 128:256, :] for c in chunks], axis=1),
                jnp.ones((ONES, 128 * len(chunks)), jnp.bfloat16),
            ],
            axis=0,
        )
        places = [place(*s) for s in sources]
        bias = [[jnp.where(pk <= own_place[i], 0.0, NEG).astype(jnp.float32) for pk in places] for i in range(2)]

        def scores(t):
            return lax.dot_general(keys, queries(t), NT, preferred_element_type=jnp.float32)

        def weights(t, s):
            s = s * SCALE
            parts = [s[i * 128 : (i + 1) * 128] for i in range(len(chunks))]
            shift = [None] * len(chunks)
            if t < 8:
                shift = list(bias[t // 4])
                if first:
                    shift[t // 4] = None
                    parts[t // 4] = jnp.where(causal, parts[t // 4], NEG)
            tops = [jnp.max(x, axis=0, keepdims=True) for x in parts]
            tops = [x if b is None else x + b for x, b in zip(tops, shift)]
            now = functools.reduce(jnp.maximum, tops)
            factor = None
            if not first:
                before = top[t, 0:1]
                now = jnp.maximum(now, before)
                factor = jnp.exp2(before - now)
            top[t, 0:1] = now
            w = [jnp.exp2(x - (now if b is None else now - b)).astype(jnp.bfloat16) for x, b in zip(parts, shift)]
            return jnp.concatenate(w, axis=0), factor

        def add(t, w, factor):
            o = jnp.dot(values, w, preferred_element_type=jnp.float32)
            acc[t] = o if factor is None else acc[t] * factor + o

        s = {i: scores(tiles[i]) for i in range(min(2, len(tiles)))}
        w = {0: weights(tiles[0], s[0])}
        for i in range(len(tiles)):
            if i in between:
                event(*between[i])
            if i + 2 < len(tiles):
                s[i + 2] = scores(tiles[i + 2])
            if i + 1 < len(tiles):
                w[i + 1] = weights(tiles[i + 1], s[i + 1])
            add(tiles[i], *w[i])

    def own(tiles):
        attend(tiles, 0, (0, 1), [(z, yh), (z, 1 - yh)], first=True)

    def step(k, tiles, between=()):
        attend(tiles, k, (0, 1, 2, 3), [(z - k, yh), (z - k, 1 - yh), (z + k, yh), (z + k, 1 - yh)], between=between)

    event(1, 0, 0)
    event(1, 0, 1)
    event(1, 1, 0)
    event(1, 1, 1)
    for copy in x_copies:
        copy.wait_recv()
    q_copy.start()
    for copy in d_copies:
        copy.wait_recv()
    own([0, 1, 2, 3, 8])
    def at(k, places, last=0):
        return [(i, (k, b, h, last)) for i, (b, h) in zip(places, [(0, 0), (0, 1), (1, 0), (1, 1)])]

    early, late = [0, 1, 2, 3, 8], [4, 5, 6, 7]
    everything = [8, 4, 5, 6, 7, 0, 1, 2, 3]
    step(1, early, at(2, (1, 2, 3, 4)))
    step(2, early, at(3, (1, 2, 3, 4)))
    q_copy.wait_recv()
    own(late)
    step(1, late)
    step(2, late, [(1, (4, 0, 0)), (3, (4, 0, 1))])
    step(3, everything, [(1, (4, 1, 0)), (3, (4, 1, 1))])

    def middle_step(k, _):
        step(k, everything, at(k + 1, (2, 4, 6, 8)))
        return 0

    lax.fori_loop(4, half - 2, middle_step, 0)
    step(half - 2, everything, at(half - 1, (2, 4, 6, 8), 1))
    step(half - 1, everything)
    for b in range(2):
        for h in range(2):
            event(half, b, h, 2)

    far = [(z - half, yh), (z + half, 1 - yh)]
    attend([8, 4, 5, 6, 7], half, (0, 3), far)
    r_copies = []
    for i in range(2):
        dstage[i, 0:136] = acc[8, 0:136, i * 128 : (i + 1) * 128]
        dstage[i, 136:144] = jnp.broadcast_to(top[8, 0:1, i * 128 : (i + 1) * 128], (8, 128))
        r_copies.append(remote(dstage.at[i], din.at[yh], r_send.at[i], r_recv.at[i], helpers[i]))
        r_copies[i].start()

    o_copies = []
    for item in (1, 0):
        if item == 0:
            attend([0, 1, 2, 3], half, (0, 3), far)
        for t in range(4):
            a = acc[item * 4 + t]
            o = a[0:128] * (1.0 / a[128:129])
            for h in range(2):
                col = (2 * t + h) * 128
                stage[item, :, col : col + 128] = o[:, h * 128 : (h + 1) * 128].T.astype(jnp.bfloat16)
        for k in range(tps):
            src = stage.at[item, pl.ds(pl.multiple_of(other_tp(k) * rows, rows), rows), :]
            dst = out.at[0, yh, :, pl.ds(pl.multiple_of(tp * 1024, 1024), 1024)]
            if item == 0 and k == 0:
                local = pltpu.make_async_copy(src, dst, o_local)
                local.start()
            else:
                o_copies.append(remote(src, dst, o_send.at[item, k], o_recv.at[item, k], owners[item][k]))
                o_copies[-1].start()

    for copy in r_copies:
        copy.wait_recv()
    wanted = jnp.zeros((1, 128), jnp.int32)
    for r in range(8):
        wanted = jnp.where(lane_row == r, row_prompt[0, r], wanted)
    shared = jnp.where(wanted == 1, din[1], din[0])
    highest = jnp.maximum(shared[136:137], dloc[136:137])
    fa, fb = jnp.exp2(shared[136:137] - highest), jnp.exp2(dloc[136:137] - highest)
    total = shared[128:129] * fa + dloc[128:129] * fb
    o = ((shared[0:128] * fa + dloc[0:128] * fb) * (1.0 / total)).T.astype(jnp.bfloat16)
    for h in range(8):
        dout[:, h * 128 : (h + 1) * 128] = o[h * 16 : (h + 1) * 16]

    for copy in x_copies + near_copies[0] + near_copies[1] + d_copies + [q_copy] + r_copies:
        copy.wait_send()
    for c in range(4):

        def drain(k, _, c=c):
            for h in range(2):
                ring(k, c, h).wait_send()
            return 0

        lax.fori_loop(1 if c in (0, 2) else 2, half + 1 if c in (0, 3) else half, drain, 0)
    local.wait()
    for copy in o_copies:
        copy.wait()


def finish(prefill, decode, prefill_out, decode_out, held, rows, shaped, in_sem, out_sem):
    pieces = prefill.shape[1]
    moves = [
        (
            pltpu.make_async_copy(prefill.at[0, i], held.at[i], in_sem.at[i]),
            pltpu.make_async_copy(held.at[i], prefill_out.at[0, i], out_sem.at[i]),
        )
        for i in range(pieces)
    ]
    moves.append(
        (
            pltpu.make_async_copy(decode, rows, in_sem.at[pieces]),
            pltpu.make_async_copy(shaped, decode_out.at[0], out_sem.at[pieces]),
        )
    )
    for load, _ in moves:
        load.start()
    for load, store in moves[:-1]:
        load.wait()
        store.start()
    load, store = moves[-1]
    load.wait()
    shaped[...] = rows[...].astype(jnp.float32).reshape(shaped.shape).astype(jnp.bfloat16)
    store.start()
    for _, store in moves:
        store.wait()


def per_device(zs, tps, prompt_query, prompt_kv, block_order, decode_query, history_kv, new_kv, hist_len, row_prompt):
    half = zs // 2
    rows = 128 // tps
    vmem = pl.BlockSpec(memory_space=pltpu.VMEM)
    anywhere = pl.BlockSpec(memory_space=pl.ANY)
    dma = pltpu.SemaphoreType.DMA
    prefill_out, decode_out = pl.pallas_call(
        functools.partial(kernel, half, tps),
        out_shape=(
            jax.ShapeDtypeStruct((1, 2, rows, 1024 * tps), jnp.bfloat16),
            jax.ShapeDtypeStruct((16, 1024), jnp.bfloat16),
        ),
        in_specs=[anywhere] * 8,
        out_specs=(anywhere, vmem),
        scratch_shapes=[
            pltpu.SMEM(block_order.shape, jnp.int32),
            pltpu.SMEM(hist_len.shape, jnp.int32),
            pltpu.SMEM(row_prompt.shape, jnp.int32),
            pltpu.VMEM((128, 1024), jnp.bfloat16),
            pltpu.VMEM((2, 128, 128), jnp.bfloat16),
            pltpu.VMEM((8, 2, 1024), jnp.bfloat16),
            pltpu.VMEM((2, 8, 64, 128), jnp.bfloat16),
            pltpu.VMEM((2, 16, 128), jnp.bfloat16),
            pltpu.VMEM((half + 1, 4, 256, 128), jnp.bfloat16),
            pltpu.VMEM((128, 128), jnp.bfloat16),
            pltpu.VMEM((128, 1024), jnp.bfloat16),
            pltpu.VMEM((128, 128), jnp.bfloat16),
            pltpu.VMEM((2, 128, 128), jnp.bfloat16),
            pltpu.VMEM((9, 128 + ONES, 256), jnp.float32),
            pltpu.VMEM((9, 8, 256), jnp.float32),
            pltpu.VMEM((2, 128, 1024), jnp.bfloat16),
            pltpu.VMEM((2, 144, 128), jnp.float32),
            pltpu.VMEM((2, 144, 128), jnp.float32),
            pltpu.VMEM((144, 128), jnp.float32),
            dma((9,)),
            dma((half + 1, 4, 2)),
            dma((half + 1, 4, 2)),
            dma((2,)),
            dma((2,)),
            dma((2, 2)),
            dma(()),
            dma(()),
            dma((2,)),
            dma((2,)),
            dma((2,)),
            dma((2,)),
            dma((2, tps)),
            dma((2, tps)),
            dma(()),
        ],
        compiler_params=pltpu.CompilerParams(
            collective_id=0, has_side_effects=True, vmem_limit_bytes=63_400_000
        ),
    )(
        block_order,
        hist_len,
        row_prompt,
        prompt_query,
        prompt_kv,
        decode_query,
        history_kv,
        new_kv.reshape(2, 16, 128),
    )
    return pl.pallas_call(
        finish,
        out_shape=(
            jax.ShapeDtypeStruct(prefill_out.shape, jnp.bfloat16),
            jax.ShapeDtypeStruct(decode_query.shape, jnp.bfloat16),
        ),
        in_specs=[anywhere] * 2,
        out_specs=(anywhere, anywhere),
        scratch_shapes=[
            pltpu.VMEM(prefill_out.shape[1:], jnp.bfloat16),
            pltpu.VMEM(decode_out.shape, jnp.bfloat16),
            pltpu.VMEM(decode_query.shape[1:], jnp.bfloat16),
            dma((3,)),
            dma((3,)),
        ],
    )(prefill_out, decode_out)


def solution(mesh):
    placed = (
        P("pool", None, "ctx", "tp"),
        P("pool", None, None, "ctx", "tp"),
        P("pool", None, None),
        P("pool", "ctx", None, "tp"),
        P("pool", None, "ctx", None, "tp"),
        P("pool", None, "ctx", None, "tp"),
        P("pool", "ctx"),
        P("pool", "ctx"),
    )
    return jax.shard_map(
        functools.partial(per_device, mesh.shape["ctx"] // 2, mesh.shape["tp"]),
        mesh=mesh,
        in_specs=placed,
        out_specs=(P("pool", None, ("ctx", "tp"), None), P("pool", "ctx", None, "tp")),
        check_vma=False,
    )
```

```python
import functools

import jax
import jax.numpy as jnp
from jax import lax
from jax.experimental import pallas as pl
from jax.experimental.pallas import tpu as pltpu
from jax.sharding import PartitionSpec as P

HEAD_SIZE = 128
NEG = -1e30
SCALE = 1.4426950408889634 / HEAD_SIZE**0.5
NT = (((1,), (1,)), ((), ()))
TN = (((0,), (0,)), ((), ()))
MESH = pl.DeviceIdType.MESH
ONES = 16


def kernel(
    half,
    tps,
    order_in,
    hist_len_in,
    row_prompt_in,
    pq,
    pkv_in,
    dq_in,
    hist_in,
    new_in,
    out,
    dout,
    order,
    hist_len,
    row_prompt,
    q0,
    raw,
    dq,
    hist,
    new,
    buf,
    psend,
    q1,
    dqs,
    dqr,
    acc,
    top,
    stage,
    dstage,
    din,
    dloc,
    in_sem,
    ring_send,
    ring_recv,
    x_send,
    x_recv,
    near_send,
    q_send,
    q_recv,
    d_send,
    d_recv,
    r_send,
    r_recv,
    o_send,
    o_recv,
    o_local,
    hello,
):
    ctx, tp, core = lax.axis_index("ctx"), lax.axis_index("tp"), lax.axis_index("pool")
    zs = 2 * half
    z, yh = ctx // 2, ctx % 2
    rows = 128 // tps

    def dev(z_, yh_, tp_, core_):
        return {"ctx": lax.rem(z_ + zs, zs) * 2 + yh_, "tp": tp_, "pool": core_}

    right, left = dev(z + 1, yh, tp, core), dev(z - 1, yh, tp, core)
    partner = dev(z, 1 - yh, tp, core)
    partner_right, partner_left = dev(z + 1, 1 - yh, tp, core), dev(z - 1, 1 - yh, tp, core)
    helpers = (dev(z, yh, tp, 1 - core), dev(z, 1 - yh, tp, 1 - core))

    def other_tp(k):
        return lax.rem(tp + k, tps)

    owners = [[dev(z, yh, other_tp(k), core) for k in range(tps)], [dev(z, 1 - yh, other_tp(k), core) for k in range(tps)]]

    def remote(src, dst, send, recv, device):
        return pltpu.make_async_remote_copy(
            src_ref=src, dst_ref=dst, send_sem=send, recv_sem=recv, device_id=device, device_id_type=MESH
        )

    fetches = [
        pltpu.make_async_copy(src, dst, in_sem.at[i])
        for i, (src, dst) in enumerate(
            [
                (pkv_in.at[0, 1], raw),
                (dq_in.at[0], dq),
                (pkv_in.at[0, 0, yh], buf.at[0, 0, 0:128]),
                (hist_len_in, hist_len),
                (hist_in.at[0], hist),
                (new_in, new),
                (order_in, order),
                (row_prompt_in, row_prompt),
                (pq.at[0, yh], q0),
            ]
        )
    ]
    for fetch in fetches:
        fetch.start()

    barrier = pltpu.get_barrier_semaphore()
    beside = [dev(z, yh, lax.rem(tp + k, tps), core) for k in (2, 6)] + [dev(z, yh, tp + 1 - 2 * (tp % 2), core), partner]
    peers = [right, left, partner_right, partner_left, *helpers, *beside]
    for peer in peers:
        pl.semaphore_signal(barrier, inc=1, device_id=peer, device_id_type=MESH)

    pl.semaphore_wait(barrier, len(peers))

    def part(ref, h):
        return ref.at[h * 128 : (h + 1) * 128]

    def ring(k, c, h, src=None):
        return remote(
            part(buf.at[k - 1, c], h) if src is None else src,
            part(buf.at[k, c], h),
            ring_send.at[k, c, h],
            ring_recv.at[k, c, h],
            right if c < 2 else left,
        )

    mine = (pkv_in.at[0, 0, yh], part(buf.at[0, 0], 1))
    theirs = (pkv_in.at[0, 0, 1 - yh], psend)
    x_copies = [remote(theirs[h], part(buf.at[0, 1], h), x_send.at[h], x_recv.at[h], partner) for h in range(2)]
    near_copies = [
        [
            remote(theirs[h], part(buf.at[1, c], h), near_send.at[i, h], ring_recv.at[1, c, h], device)
            for i, (c, device) in enumerate([(1, partner_right), (3, partner_left)])
        ]
        for h in range(2)
    ]
    q_copy = remote(pq.at[0, 1 - yh], q1, q_send, q_recv, partner)
    d_copies = [remote(dqs, dqr.at[i], d_send.at[i], d_recv.at[i], helpers[i]) for i in range(2)]
    def greet(i):
        if i:
            pl.semaphore_wait(hello.at[i - 1], len(beside))
        if i < 3:
            for peer in beside:
                pl.semaphore_signal(hello.at[i], inc=1, device_id=peer, device_id_type=MESH)

    def send_own(h):
        for copy in [ring(1, 0, h, mine[h]), ring(1, 2, h, mine[h]), *near_copies[h], x_copies[h]]:
            copy.start()

    send_own(0)
    fetches[0].wait()
    buf[0, 0, 128:256, :] = raw[yh].astype(jnp.float32).T.astype(jnp.bfloat16)
    psend[...] = raw[1 - yh].astype(jnp.float32).T.astype(jnp.bfloat16)
    send_own(1)
    greet(0)
    fetches[1].wait()
    wide = dq[...].astype(jnp.float32).reshape(16, 1024)
    dqt = jnp.concatenate([wide[:, h * 128 : (h + 1) * 128] for h in range(8)], axis=0).astype(jnp.bfloat16)
    dqs[...] = dqt
    for copy in d_copies:
        copy.start()
    for fetch in fetches[2:]:
        fetch.wait()

    lane = lax.broadcasted_iota(jnp.int32, (1, 128), 1)
    lane_row, lane_step = lax.rem(lane, 16) // 2, lax.rem(lane, 2)
    hs = lax.dot_general(hist[0].reshape(512, 128), dqt, NT, preferred_element_type=jnp.float32) * SCALE
    key_in_row = lax.broadcasted_iota(jnp.int32, (64, 128), 0)
    hs = jnp.concatenate(
        [
            jnp.where((lane_row == r) & (key_in_row < hist_len[0, r]), hs[r * 64 : (r + 1) * 64], NEG)
            for r in range(8)
        ],
        axis=0,
    )
    ns = lax.dot_general(new[0], dqt, NT, preferred_element_type=jnp.float32) * SCALE
    key = lax.broadcasted_iota(jnp.int32, (16, 128), 0)
    ns = jnp.where((key // 2 == lane_row) & (lax.rem(key, 2) <= lane_step), ns, NEG)
    highest = jnp.maximum(jnp.max(hs, axis=0, keepdims=True), jnp.max(ns, axis=0, keepdims=True))
    hw, nw = jnp.exp2(hs - highest), jnp.exp2(ns - highest)
    weighted = lax.dot_general(
        hist[1].reshape(512, 128), hw.astype(jnp.bfloat16), TN, preferred_element_type=jnp.float32
    ) + lax.dot_general(new[1], nw.astype(jnp.bfloat16), TN, preferred_element_type=jnp.float32)
    dloc[0:128] = weighted
    dloc[128:136] = jnp.broadcast_to(jnp.sum(hw, 0, keepdims=True) + jnp.sum(nw, 0, keepdims=True), (8, 128))
    dloc[136:144] = jnp.broadcast_to(highest, (8, 128))

    def event(k, b, h, last=0):
        for c in (b, b + 2):
            if last < 2 or c in (0, 3):
                ring(k, c, h).wait_recv()
                if last == 0 or (last == 1 and c in (0, 3)):
                    ring(k + 1, c, h).start()

    def queries(t):
        if t == 8:
            return dqr[...].reshape(256, 128)
        x = (q0 if t < 4 else q1)[:, t % 4 * 256 : (t % 4 + 1) * 256]
        return jnp.concatenate([x[:, :128], x[:, 128:]], axis=0)

    causal = lax.rem(lax.broadcasted_iota(jnp.int32, (128, 256), 1), 128) >= lax.broadcasted_iota(
        jnp.int32, (128, 256), 0
    )

    def place(z_, yh_):
        return order[0, yh, lax.rem(z_ + zs, zs) * 2 + yh_]

    own_place = (place(z, yh), place(z, 1 - yh))

    def attend(tiles, u, chunks, sources, first=False, between=()):
        between = dict(between)
        keys = jnp.concatenate([buf[u, c, 0:128, :] for c in chunks], axis=0)
        values = jnp.concatenate(
            [
                jnp.concatenate([buf[u, c, 128:256, :] for c in chunks], axis=1),
                jnp.ones((ONES, 128 * len(chunks)), jnp.bfloat16),
            ],
            axis=0,
        )
        places = [place(*s) for s in sources]
        bias = [[jnp.where(pk <= own_place[i], 0.0, NEG).astype(jnp.float32) for pk in places] for i in range(2)]

        def scores(t):
            return lax.dot_general(keys, queries(t), NT, preferred_element_type=jnp.float32)

        def weights(t, s):
            s = s * SCALE
            parts = [s[i * 128 : (i + 1) * 128] for i in range(len(chunks))]
            shift = [None] * len(chunks)
            if t < 8:
                shift = list(bias[t // 4])
                if first:
                    shift[t // 4] = None
                    parts[t // 4] = jnp.where(causal, parts[t // 4], NEG)
            tops = [jnp.max(x, axis=0, keepdims=True) for x in parts]
            tops = [x if b is None else x + b for x, b in zip(tops, shift)]
            now = functools.reduce(jnp.maximum, tops)
            factor = None
            if not first:
                before = top[t, 0:1]
                now = jnp.maximum(now, before)
                factor = jnp.exp2(before - now)
            top[t, 0:1] = now
            w = [jnp.exp2(x - (now if b is None else now - b)).astype(jnp.bfloat16) for x, b in zip(parts, shift)]
            return jnp.concatenate(w, axis=0), factor

        def add(t, w, factor):
            o = jnp.dot(values, w, preferred_element_type=jnp.float32)
            acc[t] = o if factor is None else acc[t] * factor + o

        s = {i: scores(tiles[i]) for i in range(min(2, len(tiles)))}
        w = {0: weights(tiles[0], s[0])}
        for i in range(len(tiles)):
            if i in between:
                event(*between[i])
            if i + 2 < len(tiles):
                s[i + 2] = scores(tiles[i + 2])
            if i + 1 < len(tiles):
                w[i + 1] = weights(tiles[i + 1], s[i + 1])
            add(tiles[i], *w[i])

    def own(tiles):
        attend(tiles, 0, (0, 1), [(z, yh), (z, 1 - yh)], first=True)

    def step(k, tiles, between=()):
        attend(tiles, k, (0, 1, 2, 3), [(z - k, yh), (z - k, 1 - yh), (z + k, yh), (z + k, 1 - yh)], between=between)

    for h in range(2):
        for b in range(2):
            event(1, b, h)
    for copy in x_copies:
        copy.wait_recv()
    q_copy.start()
    for copy in d_copies:
        copy.wait_recv()
    own([0, 1, 2, 3, 8])
    def at(k, places, last=0):
        return [(i, (k, b, h, last)) for i, (b, h) in zip(places, [(0, 0), (1, 0), (0, 1), (1, 1)])]

    early, late = [0, 1, 2, 3, 8], [4, 5, 6, 7]
    everything = [8, 4, 5, 6, 7, 0, 1, 2, 3]
    step(1, early, at(2, (1, 2, 3, 4)))
    greet(1)
    step(2, early, at(3, (1, 2, 3, 4)))
    q_copy.wait_recv()
    own(late)
    step(1, late)
    greet(2)
    step(2, late, at(4, (1, 3)))
    step(3, everything, [(1, (4, 0, 1)), (3, (4, 1, 1))])

    def middle_step(k, _):
        step(k, everything, at(k + 1, (2, 4, 6, 8)))
        return 0

    lax.fori_loop(4, half - 2, middle_step, 0)
    step(half - 2, everything, at(half - 1, (2, 4, 6, 8), 1))
    step(half - 1, everything)
    for b in range(2):
        for h in range(2):
            event(half, b, h, 2)

    far = [(z - half, yh), (z + half, 1 - yh)]
    attend([8, 4, 5, 6, 7], half, (0, 3), far)
    r_copies = []
    for i in range(2):
        dstage[i, 0:136] = acc[8, 0:136, i * 128 : (i + 1) * 128]
        dstage[i, 136:144] = jnp.broadcast_to(top[8, 0:1, i * 128 : (i + 1) * 128], (8, 128))
        r_copies.append(remote(dstage.at[i], din.at[yh], r_send.at[i], r_recv.at[i], helpers[i]))
        r_copies[i].start()

    o_copies = []
    greet(3)
    for item in (1, 0):
        if item == 0:
            attend([0, 1, 2, 3], half, (0, 3), far)
        for t in range(4):
            a = acc[item * 4 + t]
            o = (a[0:128] * (1.0 / a[128:129])).astype(jnp.bfloat16)
            for h in range(2):
                col = (2 * t + h) * 128
                stage[item, :, col : col + 128] = o[:, h * 128 : (h + 1) * 128].T
        for k in range(tps):
            src = stage.at[item, pl.ds(pl.multiple_of(other_tp(k) * rows, rows), rows), :]
            dst = out.at[0, yh, :, pl.ds(pl.multiple_of(tp * 1024, 1024), 1024)]
            if item == 0 and k == 0:
                local = pltpu.make_async_copy(src, dst, o_local)
                local.start()
            else:
                o_copies.append(remote(src, dst, o_send.at[item, k], o_recv.at[item, k], owners[item][k]))
                o_copies[-1].start()

    for copy in r_copies:
        copy.wait_recv()
    wanted = jnp.zeros((1, 128), jnp.int32)
    for r in range(8):
        wanted = jnp.where(lane_row == r, row_prompt[0, r], wanted)
    shared = jnp.where(wanted == 1, din[1], din[0])
    highest = jnp.maximum(shared[136:137], dloc[136:137])
    fa, fb = jnp.exp2(shared[136:137] - highest), jnp.exp2(dloc[136:137] - highest)
    total = shared[128:129] * fa + dloc[128:129] * fb
    o = ((shared[0:128] * fa + dloc[0:128] * fb) * (1.0 / total)).T.astype(jnp.bfloat16)
    for h in range(8):
        dout[:, h * 128 : (h + 1) * 128] = o[h * 16 : (h + 1) * 16]

    for copy in x_copies + near_copies[0] + near_copies[1] + d_copies + [q_copy] + r_copies:
        copy.wait_send()
    for c in range(4):

        def drain(k, _, c=c):
            for h in range(2):
                ring(k, c, h).wait_send()
            return 0

        lax.fori_loop(1 if c in (0, 2) else 2, half + 1 if c in (0, 3) else half, drain, 0)
    local.wait()
    for copy in o_copies:
        copy.wait()


def finish(prefill, decode, prefill_out, decode_out, held, rows, shaped, in_sem, out_sem):
    pieces = prefill.shape[1]
    moves = [
        (
            pltpu.make_async_copy(prefill.at[0, i], held.at[i], in_sem.at[i]),
            pltpu.make_async_copy(held.at[i], prefill_out.at[0, i], out_sem.at[i]),
        )
        for i in range(pieces)
    ]
    moves.append(
        (
            pltpu.make_async_copy(decode, rows, in_sem.at[pieces]),
            pltpu.make_async_copy(shaped, decode_out.at[0], out_sem.at[pieces]),
        )
    )
    for load, _ in moves:
        load.start()
    for load, store in moves[:-1]:
        load.wait()
        store.start()
    load, store = moves[-1]
    load.wait()
    shaped[...] = rows[...].astype(jnp.float32).reshape(shaped.shape).astype(jnp.bfloat16)
    store.start()
    for _, store in moves:
        store.wait()


def per_device(zs, tps, prompt_query, prompt_kv, block_order, decode_query, history_kv, new_kv, hist_len, row_prompt):
    half = zs // 2
    rows = 128 // tps
    vmem = pl.BlockSpec(memory_space=pltpu.VMEM)
    anywhere = pl.BlockSpec(memory_space=pl.ANY)
    dma = pltpu.SemaphoreType.DMA
    prefill_out, decode_out = pl.pallas_call(
        functools.partial(kernel, half, tps),
        out_shape=(
            jax.ShapeDtypeStruct((1, 2, rows, 1024 * tps), jnp.bfloat16),
            jax.ShapeDtypeStruct((16, 1024), jnp.bfloat16),
        ),
        in_specs=[anywhere] * 8,
        out_specs=(anywhere, vmem),
        scratch_shapes=[
            pltpu.SMEM(block_order.shape, jnp.int32),
            pltpu.SMEM(hist_len.shape, jnp.int32),
            pltpu.SMEM(row_prompt.shape, jnp.int32),
            pltpu.VMEM((128, 1024), jnp.bfloat16),
            pltpu.VMEM((2, 128, 128), jnp.bfloat16),
            pltpu.VMEM((8, 2, 1024), jnp.bfloat16),
            pltpu.VMEM((2, 8, 64, 128), jnp.bfloat16),
            pltpu.VMEM((2, 16, 128), jnp.bfloat16),
            pltpu.VMEM((half + 1, 4, 256, 128), jnp.bfloat16),
            pltpu.VMEM((128, 128), jnp.bfloat16),
            pltpu.VMEM((128, 1024), jnp.bfloat16),
            pltpu.VMEM((128, 128), jnp.bfloat16),
            pltpu.VMEM((2, 128, 128), jnp.bfloat16),
            pltpu.VMEM((9, 128 + ONES, 256), jnp.float32),
            pltpu.VMEM((9, 8, 256), jnp.float32),
            pltpu.VMEM((2, 128, 1024), jnp.bfloat16),
            pltpu.VMEM((2, 144, 128), jnp.float32),
            pltpu.VMEM((2, 144, 128), jnp.float32),
            pltpu.VMEM((144, 128), jnp.float32),
            dma((9,)),
            dma((half + 1, 4, 2)),
            dma((half + 1, 4, 2)),
            dma((2,)),
            dma((2,)),
            dma((2, 2)),
            dma(()),
            dma(()),
            dma((2,)),
            dma((2,)),
            dma((2,)),
            dma((2,)),
            dma((2, tps)),
            dma((2, tps)),
            dma(()),
            pltpu.SemaphoreType.REGULAR((3,)),
        ],
        compiler_params=pltpu.CompilerParams(
            collective_id=0, has_side_effects=True, vmem_limit_bytes=63_400_000
        ),
    )(
        block_order,
        hist_len,
        row_prompt,
        prompt_query,
        prompt_kv,
        decode_query,
        history_kv,
        new_kv.reshape(2, 16, 128),
    )
    return pl.pallas_call(
        finish,
        out_shape=(
            jax.ShapeDtypeStruct(prefill_out.shape, jnp.bfloat16),
            jax.ShapeDtypeStruct(decode_query.shape, jnp.bfloat16),
        ),
        in_specs=[anywhere] * 2,
        out_specs=(anywhere, anywhere),
        scratch_shapes=[
            pltpu.VMEM(prefill_out.shape[1:], jnp.bfloat16),
            pltpu.VMEM(decode_out.shape, jnp.bfloat16),
            pltpu.VMEM(decode_query.shape[1:], jnp.bfloat16),
            dma((3,)),
            dma((3,)),
        ],
    )(prefill_out, decode_out)


def solution(mesh):
    placed = (
        P("pool", None, "ctx", "tp"),
        P("pool", None, None, "ctx", "tp"),
        P("pool", None, None),
        P("pool", "ctx", None, "tp"),
        P("pool", None, "ctx", None, "tp"),
        P("pool", None, "ctx", None, "tp"),
        P("pool", "ctx"),
        P("pool", "ctx"),
    )
    return jax.shard_map(
        functools.partial(per_device, mesh.shape["ctx"] // 2, mesh.shape["tp"]),
        mesh=mesh,
        in_specs=placed,
        out_specs=(P("pool", None, ("ctx", "tp"), None), P("pool", "ctx", None, "tp")),
        check_vma=False,
    )
```

```python
import functools

import jax
import jax.numpy as jnp
from jax import lax
from jax.experimental import pallas as pl
from jax.experimental.pallas import tpu as pltpu
from jax.sharding import PartitionSpec as P

HEAD_SIZE = 128
NEG = -1e30
SCALE = 1.4426950408889634 / HEAD_SIZE**0.5
NT = (((1,), (1,)), ((), ()))
TN = (((0,), (0,)), ((), ()))
MESH = pl.DeviceIdType.MESH
ONES = 16


def kernel(
    half,
    tps,
    order_in,
    hist_len_in,
    row_prompt_in,
    pq,
    pkv_in,
    dq_in,
    hist_in,
    new_in,
    out,
    dout,
    order,
    hist_len,
    row_prompt,
    q0,
    raw,
    dq,
    hist,
    new,
    buf,
    psend,
    q1,
    dqs,
    dqr,
    acc,
    top,
    stage,
    dstage,
    din,
    dloc,
    in_sem,
    ring_send,
    ring_recv,
    x_send,
    x_recv,
    near_send,
    q_send,
    q_recv,
    d_send,
    d_recv,
    r_send,
    r_recv,
    o_send,
    o_recv,
    o_local,
    hello,
    dheld,
    dout_sem,
):
    ctx, tp, core = lax.axis_index("ctx"), lax.axis_index("tp"), lax.axis_index("pool")
    zs = 2 * half
    z, yh = ctx // 2, ctx % 2
    rows = 128 // tps

    def dev(z_, yh_, tp_, core_):
        return {"ctx": lax.rem(z_ + zs, zs) * 2 + yh_, "tp": tp_, "pool": core_}

    right, left = dev(z + 1, yh, tp, core), dev(z - 1, yh, tp, core)
    partner = dev(z, 1 - yh, tp, core)
    partner_right, partner_left = dev(z + 1, 1 - yh, tp, core), dev(z - 1, 1 - yh, tp, core)
    helpers = (dev(z, yh, tp, 1 - core), dev(z, 1 - yh, tp, 1 - core))

    def other_tp(k):
        return lax.rem(tp + k, tps)

    owners = [[dev(z, yh, other_tp(k), core) for k in range(tps)], [dev(z, 1 - yh, other_tp(k), core) for k in range(tps)]]

    def remote(src, dst, send, recv, device):
        return pltpu.make_async_remote_copy(
            src_ref=src, dst_ref=dst, send_sem=send, recv_sem=recv, device_id=device, device_id_type=MESH
        )

    fetches = [
        pltpu.make_async_copy(src, dst, in_sem.at[i])
        for i, (src, dst) in enumerate(
            [
                (pkv_in.at[0, 1], raw),
                (dq_in.at[0], dq),
                (pkv_in.at[0, 0, yh], buf.at[0, 0, 0:128]),
                (hist_len_in, hist_len),
                (hist_in.at[0], hist),
                (new_in, new),
                (order_in, order),
                (row_prompt_in, row_prompt),
                (pq.at[0, yh], q0),
            ]
        )
    ]
    for fetch in fetches:
        fetch.start()

    barrier = pltpu.get_barrier_semaphore()
    beside = [dev(z, yh, lax.rem(tp + k, tps), core) for k in (2, 6)] + [dev(z, yh, tp + 1 - 2 * (tp % 2), core), partner]
    peers = [right, left, partner_right, partner_left, *helpers, *beside]
    for peer in peers:
        pl.semaphore_signal(barrier, inc=1, device_id=peer, device_id_type=MESH)

    pl.semaphore_wait(barrier, len(peers))

    def part(ref, h):
        return ref.at[h * 128 : (h + 1) * 128]

    def ring(k, c, h, src=None):
        return remote(
            part(buf.at[k - 1, c], h) if src is None else src,
            part(buf.at[k, c], h),
            ring_send.at[k, c, h],
            ring_recv.at[k, c, h],
            right if c < 2 else left,
        )

    mine = (pkv_in.at[0, 0, yh], part(buf.at[0, 0], 1))
    theirs = (pkv_in.at[0, 0, 1 - yh], psend)
    x_copies = [remote(theirs[h], part(buf.at[0, 1], h), x_send.at[h], x_recv.at[h], partner) for h in range(2)]
    near_copies = [
        [
            remote(theirs[h], part(buf.at[1, c], h), near_send.at[i, h], ring_recv.at[1, c, h], device)
            for i, (c, device) in enumerate([(1, partner_right), (3, partner_left)])
        ]
        for h in range(2)
    ]
    q_copy = remote(pq.at[0, 1 - yh], q1, q_send, q_recv, partner)
    d_copies = [remote(dqs, dqr.at[i], d_send.at[i], d_recv.at[i], helpers[i]) for i in range(2)]
    def greet(i):
        if i:
            pl.semaphore_wait(hello.at[i - 1], len(beside))
        if i < 3:
            for peer in beside:
                pl.semaphore_signal(hello.at[i], inc=1, device_id=peer, device_id_type=MESH)

    def send_own(h):
        for copy in [ring(1, 0, h, mine[h]), ring(1, 2, h, mine[h]), *near_copies[h], x_copies[h]]:
            copy.start()

    send_own(0)
    fetches[0].wait()
    buf[0, 0, 128:256, :] = raw[yh].astype(jnp.float32).T.astype(jnp.bfloat16)
    psend[...] = raw[1 - yh].astype(jnp.float32).T.astype(jnp.bfloat16)
    send_own(1)
    greet(0)
    fetches[1].wait()
    wide = dq[...].astype(jnp.float32).reshape(16, 1024)
    dqt = jnp.concatenate([wide[:, h * 128 : (h + 1) * 128] for h in range(8)], axis=0).astype(jnp.bfloat16)
    dqs[...] = dqt
    for copy in d_copies:
        copy.start()
    for fetch in fetches[2:]:
        fetch.wait()

    lane = lax.broadcasted_iota(jnp.int32, (1, 128), 1)
    lane_row, lane_step = lax.rem(lane, 16) // 2, lax.rem(lane, 2)
    hs = lax.dot_general(hist[0].reshape(512, 128), dqt, NT, preferred_element_type=jnp.float32) * SCALE
    key_in_row = lax.broadcasted_iota(jnp.int32, (64, 128), 0)
    hs = jnp.concatenate(
        [
            jnp.where((lane_row == r) & (key_in_row < hist_len[0, r]), hs[r * 64 : (r + 1) * 64], NEG)
            for r in range(8)
        ],
        axis=0,
    )
    ns = lax.dot_general(new[0], dqt, NT, preferred_element_type=jnp.float32) * SCALE
    key = lax.broadcasted_iota(jnp.int32, (16, 128), 0)
    ns = jnp.where((key // 2 == lane_row) & (lax.rem(key, 2) <= lane_step), ns, NEG)
    highest = jnp.maximum(jnp.max(hs, axis=0, keepdims=True), jnp.max(ns, axis=0, keepdims=True))
    hw, nw = jnp.exp2(hs - highest), jnp.exp2(ns - highest)
    weighted = lax.dot_general(
        hist[1].reshape(512, 128), hw.astype(jnp.bfloat16), TN, preferred_element_type=jnp.float32
    ) + lax.dot_general(new[1], nw.astype(jnp.bfloat16), TN, preferred_element_type=jnp.float32)
    dloc[0:128] = weighted
    dloc[128:136] = jnp.broadcast_to(jnp.sum(hw, 0, keepdims=True) + jnp.sum(nw, 0, keepdims=True), (8, 128))
    dloc[136:144] = jnp.broadcast_to(highest, (8, 128))

    def event(k, b, h, last=0):
        for c in (b, b + 2):
            if last < 2 or c in (0, 3):
                ring(k, c, h).wait_recv()
                if last == 0 or (last == 1 and c in (0, 3)):
                    ring(k + 1, c, h).start()

    def queries(t):
        if t == 8:
            return dqr[...].reshape(256, 128)
        x = (q0 if t < 4 else q1)[:, t % 4 * 256 : (t % 4 + 1) * 256]
        return jnp.concatenate([x[:, :128], x[:, 128:]], axis=0)

    causal = lax.rem(lax.broadcasted_iota(jnp.int32, (128, 256), 1), 128) >= lax.broadcasted_iota(
        jnp.int32, (128, 256), 0
    )

    def place(z_, yh_):
        return order[0, yh, lax.rem(z_ + zs, zs) * 2 + yh_]

    own_place = (place(z, yh), place(z, 1 - yh))

    def attend(tiles, u, chunks, sources, first=False, between=(), after=None):
        between = dict(between)
        keys = jnp.concatenate([buf[u, c, 0:128, :] for c in chunks], axis=0)
        values = jnp.concatenate(
            [
                jnp.concatenate([buf[u, c, 128:256, :] for c in chunks], axis=1),
                jnp.ones((ONES, 128 * len(chunks)), jnp.bfloat16),
            ],
            axis=0,
        )
        places = [place(*s) for s in sources]
        bias = [[jnp.where(pk <= own_place[i], 0.0, NEG).astype(jnp.float32) for pk in places] for i in range(2)]

        def scores(t):
            return lax.dot_general(keys, queries(t), NT, preferred_element_type=jnp.float32)

        def weights(t, s):
            s = s * SCALE
            parts = [s[i * 128 : (i + 1) * 128] for i in range(len(chunks))]
            shift = [None] * len(chunks)
            if t < 8:
                shift = list(bias[t // 4])
                if first:
                    shift[t // 4] = None
                    parts[t // 4] = jnp.where(causal, parts[t // 4], NEG)
            tops = [jnp.max(x, axis=0, keepdims=True) for x in parts]
            tops = [x if b is None else x + b for x, b in zip(tops, shift)]
            now = functools.reduce(jnp.maximum, tops)
            factor = None
            if not first:
                before = top[t, 0:1]
                now = jnp.maximum(now, before)
                factor = jnp.exp2(before - now)
            top[t, 0:1] = now
            w = [jnp.exp2(x - (now if b is None else now - b)).astype(jnp.bfloat16) for x, b in zip(parts, shift)]
            return jnp.concatenate(w, axis=0), factor

        def add(t, w, factor):
            o = jnp.dot(values, w, preferred_element_type=jnp.float32)
            acc[t] = o if factor is None else acc[t] * factor + o

        s = {i: scores(tiles[i]) for i in range(min(2, len(tiles)))}
        w = {0: weights(tiles[0], s[0])}
        for i in range(len(tiles)):
            if i in between:
                event(*between[i])
            if i + 2 < len(tiles):
                s[i + 2] = scores(tiles[i + 2])
            if i + 1 < len(tiles):
                w[i + 1] = weights(tiles[i + 1], s[i + 1])
            add(tiles[i], *w[i])
            if after:
                after(tiles[i])

    def own(tiles):
        attend(tiles, 0, (0, 1), [(z, yh), (z, 1 - yh)], first=True)

    def step(k, tiles, between=()):
        attend(tiles, k, (0, 1, 2, 3), [(z - k, yh), (z - k, 1 - yh), (z + k, yh), (z + k, 1 - yh)], between=between)

    for h in range(2):
        for b in range(2):
            event(1, b, h)
        if h == 0:
            q_copy.start()
    for copy in x_copies:
        copy.wait_recv()
    for copy in d_copies:
        copy.wait_recv()
    own([0, 1, 2, 3, 8])
    def at(k, places, last=0):
        return [(i, (k, b, h, last)) for i, (b, h) in zip(places, [(0, 0), (1, 0), (0, 1), (1, 1)])]

    early, late = [0, 1, 2, 3, 8], [4, 5, 6, 7]
    everything = [8, 4, 5, 6, 7, 0, 1, 2, 3]
    step(1, early, at(2, (1, 2, 3, 4)))
    greet(1)
    step(2, early, at(3, (1, 2, 3, 4)))
    q_copy.wait_recv()
    own(late)
    step(1, late, at(4, (1, 3)))
    greet(2)
    step(2, late, [(1, (4, 0, 1)), (3, (4, 1, 1))])
    step(3, everything, at(5, (1, 3, 5, 7)))

    def middle_step(k, _):
        step(k, everything, at(k + 2, (1, 3, 5, 7)))
        return 0

    lax.fori_loop(4, half - 3, middle_step, 0)
    step(half - 3, everything, at(half - 1, (1, 3, 5, 7), 1))
    step(half - 2, everything)
    step(half - 1, everything)
    for b in range(2):
        for h in range(2):
            event(half, b, h, 2)

    far = [(z - half, yh), (z + half, 1 - yh)]
    r_copies, o_copies, local = [], [], []

    def deliver(t):
        if t == 8:
            for i in range(2):
                dstage[i, 0:136] = acc[8, 0:136, i * 128 : (i + 1) * 128]
                dstage[i, 136:144] = jnp.broadcast_to(top[8, 0:1, i * 128 : (i + 1) * 128], (8, 128))
                r_copies.append(remote(dstage.at[i], din.at[yh], r_send.at[i], r_recv.at[i], helpers[i]))
                r_copies[i].start()
            return
        item = t // 4
        a = acc[t]
        o = (a[0:128] * (1.0 / a[128:129])).astype(jnp.bfloat16)
        for h in range(2):
            col = (2 * (t % 4) + h) * 128
            stage[item, :, col : col + 128] = o[:, h * 128 : (h + 1) * 128].T
        if t == 7:
            greet(3)
        if t % 4 < 3:
            return
        for k in range(tps):
            src = stage.at[item, pl.ds(pl.multiple_of(other_tp(k) * rows, rows), rows), :]
            dst = out.at[0, yh, :, pl.ds(pl.multiple_of(tp * 1024, 1024), 1024)]
            if item == 0 and k == 0:
                local.append(pltpu.make_async_copy(src, dst, o_local))
                local[0].start()
            else:
                o_copies.append(remote(src, dst, o_send.at[item, k], o_recv.at[item, k], owners[item][k]))
                o_copies[-1].start()

    attend(everything, half, (0, 3), far, after=deliver)

    for copy in r_copies:
        copy.wait_recv()
    wanted = jnp.zeros((1, 128), jnp.int32)
    for r in range(8):
        wanted = jnp.where(lane_row == r, row_prompt[0, r], wanted)
    shared = jnp.where(wanted == 1, din[1], din[0])
    highest = jnp.maximum(shared[136:137], dloc[136:137])
    fa, fb = jnp.exp2(shared[136:137] - highest), jnp.exp2(dloc[136:137] - highest)
    total = shared[128:129] * fa + dloc[128:129] * fb
    o = ((shared[0:128] * fa + dloc[0:128] * fb) * (1.0 / total)).T
    o = jnp.concatenate([o[h * 16 : (h + 1) * 16] for h in range(8)], axis=1)
    dheld[...] = o.reshape(dheld.shape).astype(jnp.bfloat16)
    d_out = pltpu.make_async_copy(dheld, dout, dout_sem)
    d_out.start()

    for copy in x_copies + near_copies[0] + near_copies[1] + d_copies + [q_copy] + r_copies:
        copy.wait_send()
    for c in range(4):

        def drain(k, _, c=c):
            for h in range(2):
                ring(k, c, h).wait_send()
            return 0

        lax.fori_loop(1 if c in (0, 2) else 2, half + 1 if c in (0, 3) else half, drain, 0)
    local[0].wait()
    d_out.wait()
    for copy in o_copies:
        copy.wait()


def finish(prefill, decode, prefill_out, decode_out, held, rows, in_sem, out_sem):
    half = prefill.shape[3] // 2
    moves = [(decode, rows, decode_out.at[0])]
    for i in range(4):
        piece = (i // 2, slice(None), pl.ds(i % 2 * half, half))
        moves.append((prefill.at[(0, *piece)], held.at[piece], prefill_out.at[(0, *piece)]))
    loads = [pltpu.make_async_copy(src, via, in_sem.at[i]) for i, (src, via, _) in enumerate(moves)]
    stores = [pltpu.make_async_copy(via, dst, out_sem.at[i]) for i, (_, via, dst) in enumerate(moves)]
    for load in loads:
        load.start()
    for load, store in zip(loads, stores):
        load.wait()
        store.start()
    for store in stores:
        store.wait()


def per_device(zs, tps, prompt_query, prompt_kv, block_order, decode_query, history_kv, new_kv, hist_len, row_prompt):
    half = zs // 2
    rows = 128 // tps
    anywhere = pl.BlockSpec(memory_space=pl.ANY)
    dma = pltpu.SemaphoreType.DMA
    prefill_out, decode_out = pl.pallas_call(
        functools.partial(kernel, half, tps),
        out_shape=(
            jax.ShapeDtypeStruct((1, 2, rows, 1024 * tps), jnp.bfloat16),
            jax.ShapeDtypeStruct((8, 2, 1024), jnp.bfloat16),
        ),
        in_specs=[anywhere] * 8,
        out_specs=(anywhere, anywhere),
        scratch_shapes=[
            pltpu.SMEM(block_order.shape, jnp.int32),
            pltpu.SMEM(hist_len.shape, jnp.int32),
            pltpu.SMEM(row_prompt.shape, jnp.int32),
            pltpu.VMEM((128, 1024), jnp.bfloat16),
            pltpu.VMEM((2, 128, 128), jnp.bfloat16),
            pltpu.VMEM((8, 2, 1024), jnp.bfloat16),
            pltpu.VMEM((2, 8, 64, 128), jnp.bfloat16),
            pltpu.VMEM((2, 16, 128), jnp.bfloat16),
            pltpu.VMEM((half + 1, 4, 256, 128), jnp.bfloat16),
            pltpu.VMEM((128, 128), jnp.bfloat16),
            pltpu.VMEM((128, 1024), jnp.bfloat16),
            pltpu.VMEM((128, 128), jnp.bfloat16),
            pltpu.VMEM((2, 128, 128), jnp.bfloat16),
            pltpu.VMEM((9, 128 + ONES, 256), jnp.float32),
            pltpu.VMEM((9, 8, 256), jnp.float32),
            pltpu.VMEM((2, 128, 1024), jnp.bfloat16),
            pltpu.VMEM((2, 144, 128), jnp.float32),
            pltpu.VMEM((2, 144, 128), jnp.float32),
            pltpu.VMEM((144, 128), jnp.float32),
            dma((9,)),
            dma((half + 1, 4, 2)),
            dma((half + 1, 4, 2)),
            dma((2,)),
            dma((2,)),
            dma((2, 2)),
            dma(()),
            dma(()),
            dma((2,)),
            dma((2,)),
            dma((2,)),
            dma((2,)),
            dma((2, tps)),
            dma((2, tps)),
            dma(()),
            pltpu.SemaphoreType.REGULAR((3,)),
            pltpu.VMEM((8, 2, 1024), jnp.bfloat16),
            dma(()),
        ],
        compiler_params=pltpu.CompilerParams(
            collective_id=0, has_side_effects=True, vmem_limit_bytes=63_400_000
        ),
    )(
        block_order,
        hist_len,
        row_prompt,
        prompt_query,
        prompt_kv,
        decode_query,
        history_kv,
        new_kv.reshape(2, 16, 128),
    )
    return pl.pallas_call(
        finish,
        out_shape=(
            jax.ShapeDtypeStruct(prefill_out.shape, jnp.bfloat16),
            jax.ShapeDtypeStruct(decode_query.shape, jnp.bfloat16),
        ),
        in_specs=[anywhere] * 2,
        out_specs=(anywhere, anywhere),
        scratch_shapes=[
            pltpu.VMEM(prefill_out.shape[1:], jnp.bfloat16),
            pltpu.VMEM(decode_out.shape, jnp.bfloat16),
            dma((5,)),
            dma((5,)),
        ],
    )(prefill_out, decode_out)


def solution(mesh):
    placed = (
        P("pool", None, "ctx", "tp"),
        P("pool", None, None, "ctx", "tp"),
        P("pool", None, None),
        P("pool", "ctx", None, "tp"),
        P("pool", None, "ctx", None, "tp"),
        P("pool", None, "ctx", None, "tp"),
        P("pool", "ctx"),
        P("pool", "ctx"),
    )
    return jax.shard_map(
        functools.partial(per_device, mesh.shape["ctx"] // 2, mesh.shape["tp"]),
        mesh=mesh,
        in_specs=placed,
        out_specs=(P("pool", None, ("ctx", "tp"), None), P("pool", "ctx", None, "tp")),
        check_vma=False,
    )
```

```python
import functools

import jax
import jax.numpy as jnp
from jax import lax
from jax.experimental import pallas as pl
from jax.experimental.pallas import tpu as pltpu
from jax.sharding import PartitionSpec as P

HEAD_SIZE = 128
NEG = -1e30
SCALE = 1.4426950408889634 / HEAD_SIZE**0.5
NT = (((1,), (1,)), ((), ()))
TN = (((0,), (0,)), ((), ()))
MESH = pl.DeviceIdType.MESH
ONES = 16


def kernel(
    half,
    tps,
    order_in,
    hist_len_in,
    row_prompt_in,
    pq,
    pkv_in,
    dq_in,
    hist_in,
    new_in,
    out,
    dout,
    order,
    hist_len,
    row_prompt,
    q0,
    raw,
    dq,
    hist,
    new,
    buf,
    psend,
    q1,
    dqs,
    dqr,
    acc,
    top,
    stage,
    dstage,
    din,
    dloc,
    in_sem,
    ring_send,
    ring_recv,
    x_send,
    x_recv,
    near_send,
    q_send,
    q_recv,
    d_send,
    d_recv,
    r_send,
    r_recv,
    o_send,
    o_recv,
    o_local,
    hello,
    dheld,
    dout_sem,
):
    ctx, tp, core = lax.axis_index("ctx"), lax.axis_index("tp"), lax.axis_index("pool")
    zs = 2 * half
    z, yh = ctx // 2, ctx % 2
    rows = 128 // tps

    def dev(z_, yh_, tp_, core_):
        return {"ctx": lax.rem(z_ + zs, zs) * 2 + yh_, "tp": tp_, "pool": core_}

    right, left = dev(z + 1, yh, tp, core), dev(z - 1, yh, tp, core)
    partner = dev(z, 1 - yh, tp, core)
    partner_right, partner_left = dev(z + 1, 1 - yh, tp, core), dev(z - 1, 1 - yh, tp, core)
    helpers = (dev(z, yh, tp, 1 - core), dev(z, 1 - yh, tp, 1 - core))

    def other_tp(k):
        return lax.rem(tp + k, tps)

    owners = [[dev(z, yh, other_tp(k), core) for k in range(tps)], [dev(z, 1 - yh, other_tp(k), core) for k in range(tps)]]

    def remote(src, dst, send, recv, device):
        return pltpu.make_async_remote_copy(
            src_ref=src, dst_ref=dst, send_sem=send, recv_sem=recv, device_id=device, device_id_type=MESH
        )

    fetches = [
        pltpu.make_async_copy(src, dst, in_sem.at[i])
        for i, (src, dst) in enumerate(
            [
                (pkv_in.at[0, 1], raw),
                (dq_in.at[0], dq),
                (pkv_in.at[0, 0, yh], buf.at[0, 0, 0:128]),
                (hist_len_in, hist_len),
                (hist_in.at[0], hist),
                (new_in, new),
                (order_in, order),
                (row_prompt_in, row_prompt),
                (pq.at[0, yh], q0),
            ]
        )
    ]
    for fetch in fetches:
        fetch.start()

    barrier = pltpu.get_barrier_semaphore()
    beside = [dev(z, yh, lax.rem(tp + k, tps), core) for k in (2, 6)] + [dev(z, yh, tp + 1 - 2 * (tp % 2), core), partner]
    peers = [right, left, partner_right, partner_left, *helpers, *beside]
    for peer in peers:
        pl.semaphore_signal(barrier, inc=1, device_id=peer, device_id_type=MESH)

    pl.semaphore_wait(barrier, len(peers))

    def part(ref, h):
        return ref.at[h * 128 : (h + 1) * 128]

    def ring(k, c, h, src=None):
        return remote(
            part(buf.at[k - 1, c], h) if src is None else src,
            part(buf.at[k, c], h),
            ring_send.at[k, c, h],
            ring_recv.at[k, c, h],
            right if c < 2 else left,
        )

    mine = (pkv_in.at[0, 0, yh], part(buf.at[0, 0], 1))
    theirs = (pkv_in.at[0, 0, 1 - yh], psend)
    x_copies = [remote(theirs[h], part(buf.at[0, 1], h), x_send.at[h], x_recv.at[h], partner) for h in range(2)]
    near_copies = [
        [
            remote(theirs[h], part(buf.at[1, c], h), near_send.at[i, h], ring_recv.at[1, c, h], device)
            for i, (c, device) in enumerate([(1, partner_right), (3, partner_left)])
        ]
        for h in range(2)
    ]
    q_copy = remote(pq.at[0, 1 - yh], q1, q_send, q_recv, partner)
    d_copies = [remote(dqs, dqr.at[i], d_send.at[i], d_recv.at[i], helpers[i]) for i in range(2)]
    def greet(i):
        if i:
            pl.semaphore_wait(hello.at[i - 1], len(beside))
        if i < 3:
            for peer in beside:
                pl.semaphore_signal(hello.at[i], inc=1, device_id=peer, device_id_type=MESH)

    def send_own(h):
        for copy in [ring(1, 0, h, mine[h]), ring(1, 2, h, mine[h]), *near_copies[h], x_copies[h]]:
            copy.start()

    send_own(0)
    fetches[0].wait()
    buf[0, 0, 128:256, :] = raw[yh].astype(jnp.float32).T.astype(jnp.bfloat16)
    psend[...] = raw[1 - yh].astype(jnp.float32).T.astype(jnp.bfloat16)
    send_own(1)
    greet(0)
    fetches[1].wait()
    wide = dq[...].astype(jnp.float32).reshape(16, 1024)
    dqt = jnp.concatenate([wide[:, h * 128 : (h + 1) * 128] for h in range(8)], axis=0).astype(jnp.bfloat16)
    dqs[...] = dqt
    for copy in d_copies:
        copy.start()
    for fetch in fetches[2:]:
        fetch.wait()

    lane = lax.broadcasted_iota(jnp.int32, (1, 128), 1)
    lane_row, lane_step = lax.rem(lane, 16) // 2, lax.rem(lane, 2)
    hs = lax.dot_general(hist[0].reshape(512, 128), dqt, NT, preferred_element_type=jnp.float32) * SCALE
    key_in_row = lax.broadcasted_iota(jnp.int32, (64, 128), 0)
    hs = jnp.concatenate(
        [
            jnp.where((lane_row == r) & (key_in_row < hist_len[0, r]), hs[r * 64 : (r + 1) * 64], NEG)
            for r in range(8)
        ],
        axis=0,
    )
    ns = lax.dot_general(new[0], dqt, NT, preferred_element_type=jnp.float32) * SCALE
    key = lax.broadcasted_iota(jnp.int32, (16, 128), 0)
    ns = jnp.where((key // 2 == lane_row) & (lax.rem(key, 2) <= lane_step), ns, NEG)
    highest = jnp.maximum(jnp.max(hs, axis=0, keepdims=True), jnp.max(ns, axis=0, keepdims=True))
    hw, nw = jnp.exp2(hs - highest), jnp.exp2(ns - highest)
    weighted = lax.dot_general(
        hist[1].reshape(512, 128), hw.astype(jnp.bfloat16), TN, preferred_element_type=jnp.float32
    ) + lax.dot_general(new[1], nw.astype(jnp.bfloat16), TN, preferred_element_type=jnp.float32)
    dloc[0:128] = weighted
    dloc[128:136] = jnp.broadcast_to(jnp.sum(hw, 0, keepdims=True) + jnp.sum(nw, 0, keepdims=True), (8, 128))
    dloc[136:144] = jnp.broadcast_to(highest, (8, 128))

    def event(k, b, h, last=0):
        for c in (b, b + 2):
            if last < 2 or c in (0, 3):
                ring(k, c, h).wait_recv()
                if last == 0 or (last == 1 and c in (0, 3)):
                    ring(k + 1, c, h).start()

    def queries(t):
        if t == 8:
            return dqr[...].reshape(256, 128)
        x = (q0 if t < 4 else q1)[:, t % 4 * 256 : (t % 4 + 1) * 256]
        return jnp.concatenate([x[:, :128], x[:, 128:]], axis=0)

    causal = lax.rem(lax.broadcasted_iota(jnp.int32, (128, 256), 1), 128) >= lax.broadcasted_iota(
        jnp.int32, (128, 256), 0
    )

    def place(z_, yh_):
        return order[0, yh, lax.rem(z_ + zs, zs) * 2 + yh_]

    own_place = (place(z, yh), place(z, 1 - yh))

    def attend(tiles, u, chunks, sources, first=False, between=(), after=None):
        between = dict(between)
        keys = jnp.concatenate([buf[u, c, 0:128, :] for c in chunks], axis=0)
        values = jnp.concatenate(
            [
                jnp.concatenate([buf[u, c, 128:256, :] for c in chunks], axis=1),
                jnp.ones((ONES, 128 * len(chunks)), jnp.bfloat16),
            ],
            axis=0,
        )
        places = [place(*s) for s in sources]
        bias = [[jnp.where(pk <= own_place[i], 0.0, NEG).astype(jnp.float32) for pk in places] for i in range(2)]

        def scores(t):
            return lax.dot_general(keys, queries(t), NT, preferred_element_type=jnp.float32)

        def weights(t, s):
            s = s * SCALE
            parts = [s[i * 128 : (i + 1) * 128] for i in range(len(chunks))]
            shift = [None] * len(chunks)
            if t < 8:
                shift = list(bias[t // 4])
                if first:
                    shift[t // 4] = None
                    parts[t // 4] = jnp.where(causal, parts[t // 4], NEG)
            tops = [jnp.max(x, axis=0, keepdims=True) for x in parts]
            tops = [x if b is None else x + b for x, b in zip(tops, shift)]
            now = functools.reduce(jnp.maximum, tops)
            factor = None
            if not first:
                before = top[t, 0:1]
                now = jnp.maximum(now, before)
                factor = jnp.exp2(before - now)
            top[t, 0:1] = now
            w = [jnp.exp2(x - (now if b is None else now - b)).astype(jnp.bfloat16) for x, b in zip(parts, shift)]
            return jnp.concatenate(w, axis=0), factor

        def add(t, w, factor):
            o = jnp.dot(values, w, preferred_element_type=jnp.float32)
            acc[t] = o if factor is None else acc[t] * factor + o

        s = {i: scores(tiles[i]) for i in range(min(2, len(tiles)))}
        w = {0: weights(tiles[0], s[0])}
        for i in range(len(tiles)):
            if i in between:
                event(*between[i])
            if i + 2 < len(tiles):
                s[i + 2] = scores(tiles[i + 2])
            if i + 1 < len(tiles):
                w[i + 1] = weights(tiles[i + 1], s[i + 1])
            add(tiles[i], *w[i])
            if after:
                after(tiles[i])

    def own(tiles, between=()):
        attend(tiles, 0, (0, 1), [(z, yh), (z, 1 - yh)], first=True, between=between)

    def step(k, tiles, between=()):
        attend(tiles, k, (0, 1, 2, 3), [(z - k, yh), (z - k, 1 - yh), (z + k, yh), (z + k, 1 - yh)], between=between)

    for h in range(2):
        for b in range(2):
            event(1, b, h)
        if h == 0:
            q_copy.start()
    for copy in x_copies:
        copy.wait_recv()
    for copy in d_copies:
        copy.wait_recv()
    def at(k, places, last=0):
        return [(i, (k, b, h, last)) for i, (b, h) in zip(places, [(0, 0), (1, 0), (0, 1), (1, 1)])]

    early, late = [0, 1, 2, 3, 8], [4, 5, 6, 7]
    everything = [8, 4, 5, 6, 7, 0, 1, 2, 3]
    own(early, at(2, (3, 4)))
    step(1, early, [(0, (2, 0, 1)), (1, (2, 1, 1))] + at(3, (3, 4)))
    greet(1)
    step(2, early, [(0, (3, 0, 1)), (1, (3, 1, 1))])
    q_copy.wait_recv()
    own(late)
    step(1, late, at(4, (1, 3)))
    greet(2)
    step(2, late, [(1, (4, 0, 1)), (3, (4, 1, 1))])
    step(3, everything, at(5, (1, 3, 5, 7)))

    def middle_step(k, _):
        step(k, everything, at(k + 2, (1, 3, 5, 7)))
        return 0

    lax.fori_loop(4, half - 3, middle_step, 0)
    step(half - 3, everything, at(half - 1, (1, 3, 5, 7), 1))
    step(half - 2, everything)
    step(half - 1, everything)
    for b in range(2):
        for h in range(2):
            event(half, b, h, 2)

    far = [(z - half, yh), (z + half, 1 - yh)]
    r_copies, o_copies, local = [], [], []

    def deliver(t):
        if t == 8:
            for i in range(2):
                dstage[i, 0:136] = acc[8, 0:136, i * 128 : (i + 1) * 128]
                dstage[i, 136:144] = jnp.broadcast_to(top[8, 0:1, i * 128 : (i + 1) * 128], (8, 128))
                r_copies.append(remote(dstage.at[i], din.at[yh], r_send.at[i], r_recv.at[i], helpers[i]))
                r_copies[i].start()
            return
        item = t // 4
        a = acc[t]
        o = (a[0:128] * (1.0 / a[128:129])).astype(jnp.bfloat16)
        for h in range(2):
            col = (2 * (t % 4) + h) * 128
            stage[item, :, col : col + 128] = o[:, h * 128 : (h + 1) * 128].T
        if t == 7:
            greet(3)
        if t % 4 < 3:
            return
        for k in range(tps):
            src = stage.at[item, pl.ds(pl.multiple_of(other_tp(k) * rows, rows), rows), :]
            dst = out.at[0, yh, :, pl.ds(pl.multiple_of(tp * 1024, 1024), 1024)]
            if item == 0 and k == 0:
                local.append(pltpu.make_async_copy(src, dst, o_local))
                local[0].start()
            else:
                o_copies.append(remote(src, dst, o_send.at[item, k], o_recv.at[item, k], owners[item][k]))
                o_copies[-1].start()

    attend(everything, half, (0, 3), far, after=deliver)

    for copy in r_copies:
        copy.wait_recv()
    wanted = jnp.zeros((1, 128), jnp.int32)
    for r in range(8):
        wanted = jnp.where(lane_row == r, row_prompt[0, r], wanted)
    shared = jnp.where(wanted == 1, din[1], din[0])
    highest = jnp.maximum(shared[136:137], dloc[136:137])
    fa, fb = jnp.exp2(shared[136:137] - highest), jnp.exp2(dloc[136:137] - highest)
    total = shared[128:129] * fa + dloc[128:129] * fb
    o = ((shared[0:128] * fa + dloc[0:128] * fb) * (1.0 / total)).T
    o = jnp.concatenate([o[h * 16 : (h + 1) * 16] for h in range(8)], axis=1)
    dheld[...] = o.reshape(dheld.shape).astype(jnp.bfloat16)
    d_out = pltpu.make_async_copy(dheld, dout, dout_sem)
    d_out.start()

    for copy in x_copies + near_copies[0] + near_copies[1] + d_copies + [q_copy] + r_copies:
        copy.wait_send()
    for c in range(4):

        def drain(k, _, c=c):
            for h in range(2):
                ring(k, c, h).wait_send()
            return 0

        lax.fori_loop(1 if c in (0, 2) else 2, half + 1 if c in (0, 3) else half, drain, 0)
    local[0].wait()
    d_out.wait()
    for copy in o_copies:
        copy.wait()


def finish(prefill, decode, prefill_out, decode_out, held, rows, in_sem, out_sem):
    half = prefill.shape[3] // 2
    moves = [(decode, rows, decode_out.at[0])]
    for i in range(4):
        piece = (i // 2, slice(None), pl.ds(i % 2 * half, half))
        moves.append((prefill.at[(0, *piece)], held.at[piece], prefill_out.at[(0, *piece)]))
    loads = [pltpu.make_async_copy(src, via, in_sem.at[i]) for i, (src, via, _) in enumerate(moves)]
    stores = [pltpu.make_async_copy(via, dst, out_sem.at[i]) for i, (_, via, dst) in enumerate(moves)]
    for load in loads:
        load.start()
    for load, store in zip(loads, stores):
        load.wait()
        store.start()
    for store in stores:
        store.wait()


def per_device(zs, tps, prompt_query, prompt_kv, block_order, decode_query, history_kv, new_kv, hist_len, row_prompt):
    half = zs // 2
    rows = 128 // tps
    anywhere = pl.BlockSpec(memory_space=pl.ANY)
    dma = pltpu.SemaphoreType.DMA
    prefill_out, decode_out = pl.pallas_call(
        functools.partial(kernel, half, tps),
        out_shape=(
            jax.ShapeDtypeStruct((1, 2, rows, 1024 * tps), jnp.bfloat16),
            jax.ShapeDtypeStruct((8, 2, 1024), jnp.bfloat16),
        ),
        in_specs=[anywhere] * 8,
        out_specs=(anywhere, anywhere),
        scratch_shapes=[
            pltpu.SMEM(block_order.shape, jnp.int32),
            pltpu.SMEM(hist_len.shape, jnp.int32),
            pltpu.SMEM(row_prompt.shape, jnp.int32),
            pltpu.VMEM((128, 1024), jnp.bfloat16),
            pltpu.VMEM((2, 128, 128), jnp.bfloat16),
            pltpu.VMEM((8, 2, 1024), jnp.bfloat16),
            pltpu.VMEM((2, 8, 64, 128), jnp.bfloat16),
            pltpu.VMEM((2, 16, 128), jnp.bfloat16),
            pltpu.VMEM((half + 1, 4, 256, 128), jnp.bfloat16),
            pltpu.VMEM((128, 128), jnp.bfloat16),
            pltpu.VMEM((128, 1024), jnp.bfloat16),
            pltpu.VMEM((128, 128), jnp.bfloat16),
            pltpu.VMEM((2, 128, 128), jnp.bfloat16),
            pltpu.VMEM((9, 128 + ONES, 256), jnp.float32),
            pltpu.VMEM((9, 8, 256), jnp.float32),
            pltpu.VMEM((2, 128, 1024), jnp.bfloat16),
            pltpu.VMEM((2, 144, 128), jnp.float32),
            pltpu.VMEM((2, 144, 128), jnp.float32),
            pltpu.VMEM((144, 128), jnp.float32),
            dma((9,)),
            dma((half + 1, 4, 2)),
            dma((half + 1, 4, 2)),
            dma((2,)),
            dma((2,)),
            dma((2, 2)),
            dma(()),
            dma(()),
            dma((2,)),
            dma((2,)),
            dma((2,)),
            dma((2,)),
            dma((2, tps)),
            dma((2, tps)),
            dma(()),
            pltpu.SemaphoreType.REGULAR((3,)),
            pltpu.VMEM((8, 2, 1024), jnp.bfloat16),
            dma(()),
        ],
        compiler_params=pltpu.CompilerParams(
            collective_id=0, has_side_effects=True, vmem_limit_bytes=63_400_000
        ),
    )(
        block_order,
        hist_len,
        row_prompt,
        prompt_query,
        prompt_kv,
        decode_query,
        history_kv,
        new_kv.reshape(2, 16, 128),
    )
    return pl.pallas_call(
        finish,
        out_shape=(
            jax.ShapeDtypeStruct(prefill_out.shape, jnp.bfloat16),
            jax.ShapeDtypeStruct(decode_query.shape, jnp.bfloat16),
        ),
        in_specs=[anywhere] * 2,
        out_specs=(anywhere, anywhere),
        scratch_shapes=[
            pltpu.VMEM(prefill_out.shape[1:], jnp.bfloat16),
            pltpu.VMEM(decode_out.shape, jnp.bfloat16),
            dma((5,)),
            dma((5,)),
        ],
    )(prefill_out, decode_out)


def solution(mesh):
    placed = (
        P("pool", None, "ctx", "tp"),
        P("pool", None, None, "ctx", "tp"),
        P("pool", None, None),
        P("pool", "ctx", None, "tp"),
        P("pool", None, "ctx", None, "tp"),
        P("pool", None, "ctx", None, "tp"),
        P("pool", "ctx"),
        P("pool", "ctx"),
    )
    return jax.shard_map(
        functools.partial(per_device, mesh.shape["ctx"] // 2, mesh.shape["tp"]),
        mesh=mesh,
        in_specs=placed,
        out_specs=(P("pool", None, ("ctx", "tp"), None), P("pool", "ctx", None, "tp")),
        check_vma=False,
    )
```
